128 devices in a mesh: dom: 4 (over x), head: 32 (over z, y, core).
Axes of the slice: x: 4, y: 4, z: 4, core: 2. Of those that a mesh axis runs over, the one named last changes fastest.
Arguments:
- tokens: bfloat16 [24, 64, 8192], P(None, 'dom', 'head'), may hold values from -6 to 6
- parents: int32 [64], replicated, may hold values from 0 to 63, as said below
- recurrent_state: float32 [64, 128, 64, 256], P('dom', 'head'), may hold values from -6 to 6
- value_history: float32 [64, 3, 8192], P('dom', None, 'head'), may hold values from -6 to 6
- mixing_history: float32 [64, 3, 2048], P('dom', None, 'head'), may hold values from -6 to 6
- input_gain: float32 [8192], P('head'), may hold values from 0.5 to 1.5
- gate_value_weight: bfloat16 [8192, 2, 8192], P(None, None, 'head'), may hold values from -0.0625 to 0.0625
- mixing_weight: bfloat16 [8192, 2048], P(None, 'head'), may hold values from -0.0625 to 0.0625
- step_weight: bfloat16 [8192, 128], P(None, 'head'), may hold values from -0.0625 to 0.0625
- value_kernel: float32 [4, 8192], P(None, 'head'), may hold values from -3 to 3
- value_offset: float32 [8192], P('head'), may hold values from -0.5 to 0.5
- mixing_kernel: float32 [4, 2048], P(None, 'head'), may hold values from -3 to 3
- mixing_offset: float32 [2048], P('head'), may hold values from -0.5 to 0.5
- step_offset: float32 [128], P('head'), may hold values from -4 to 0
- decay_log: float32 [128], P('head'), may hold values from -2 to 1.5
- skip_gain: float32 [128], P('head'), may hold values from 0.5 to 1.5
- output_gain: float32 [8192], P('head'), may hold values from 0.5 to 1.5
- output_weight: bfloat16 [8192, 8192], P('head'), may hold values from -0.0625 to 0.0625
Outputs:
- mixed: bfloat16 [24, 64, 8192], P(None, 'dom', 'head')
The draws below stay inside these ranges and needn't reach their ends.
Inputs may be any that keep to these rules, and one draw needn't show every extreme that they name: parents comes from systematic resampling: it never falls with i, and offspring counts are very uneven, so that a particle's parent may sit several blocks of 16 particles away.
All inputs are finite; a program needn't handle non-finite values.
Results may differ from the reference program's by a relative error of at most 0.023.
Values may be sent and summed in bfloat16 or wider, within the bound.
A program may use at most 128 MiB of HBM per device.

```python
import jax
import jax.numpy as jnp
from jax import lax

D = 8192
HEADS = 128
GROUPS = 4
P_SIZE = 64
N = 256
K = 4
STEPS = 24
PARTICLES = 64


def draw_parents(key, part):
    count = PARTICLES
    key_base, key_place, key_offset = jax.random.split(key, 3)
    base_weight = jax.random.randint(key_base, (count,), 1, 64)
    quarter = count // 4
    hot_start = jax.random.randint(key_place, (), 0, count - quarter + 1)
    position = jnp.arange(count, dtype=jnp.int32)
    inside = (position >= hot_start) & (position < hot_start + quarter)
    weights = base_weight * jnp.where(inside, 16, 1)
    cumulative = jnp.cumsum(weights).astype(jnp.int32)
    grand_total = cumulative[count - 1]
    offset = jax.random.randint(key_offset, (), 0, grand_total)
    target = offset + position * grand_total
    below = cumulative[None, :] * count <= target[:, None]
    chosen = jnp.sum(below.astype(jnp.int32), axis=1).astype(jnp.int32)
    chosen = chosen.at[0].set(0)
    chosen = chosen.at[count - 1].set(count - 1)
    return chosen


def levels(key, extent, shards, smallest, high):
    def one(dim, parts):
        draws = jax.random.uniform(jax.random.fold_in(jax.random.fold_in(key, 6), dim), (parts,), jnp.float32, smallest / len(shards), high / len(shards))
        return jnp.repeat(jnp.exp(draws), extent[dim] // parts).reshape((-1,) + (1,) * (len(extent) - dim - 1))

    gain = one(*shards[0])
    for cut in shards[1:]:
        gain = gain * one(*cut)
    return gain


def noise(own_key, extent, scale, reach, cuts=(), kind=jnp.bfloat16):
    array = scale * jax.random.normal(own_key, extent, jnp.float32)
    if cuts:
        array = array * levels(own_key, extent, cuts, -0.22, 0.18)
    return jnp.clip(array, -reach, reach).astype(kind)


def setup_inputs(seed: int = 0) -> dict:
    splits = jax.random.split(jax.random.key(seed), 19)
    return {
        "tokens": noise(splits[0], (STEPS, PARTICLES, D), 1.0, 6.0, ((1, 4), (2, 32))),
        "parents": draw_parents(jax.random.fold_in(splits[18], 71), 0),
        "recurrent_state": noise(splits[2], (PARTICLES, HEADS, P_SIZE, N), 1.0, 6.0, ((0, 4), (1, 32)), jnp.float32),
        "value_history": noise(splits[3], (PARTICLES, K - 1, HEADS * P_SIZE), 1.0, 6.0, ((0, 4), (2, 32)), jnp.float32),
        "mixing_history": noise(splits[4], (PARTICLES, K - 1, 2 * GROUPS * N), 1.0, 6.0, ((0, 4), (2, 32)), jnp.float32),
        "input_gain": jnp.clip(1.0 + 0.1 * jax.random.normal(splits[5], (D,), jnp.float32), 0.5, 1.5),
        "gate_value_weight": noise(splits[6], (D, 2, HEADS * P_SIZE), D ** -0.5, 0.0625, ((2, 32),)),
        "mixing_weight": noise(splits[7], (D, 2 * GROUPS * N), D ** -0.5, 0.0625, ((1, 32),)),
        "step_weight": noise(splits[8], (D, HEADS), D ** -0.5, 0.0625, ((1, 32),)),
        "value_kernel": noise(splits[9], (K, HEADS * P_SIZE), K ** -0.5, 3.0, ((1, 32),), jnp.float32),
        "value_offset": jnp.clip(jax.random.uniform(splits[10], (HEADS * P_SIZE,), jnp.float32, -0.5, 0.5) * levels(splits[10], (HEADS * P_SIZE,), ((0, 32),), -0.4, 0.0), -0.5, 0.5),
        "mixing_kernel": noise(splits[11], (K, 2 * GROUPS * N), K ** -0.5, 3.0, ((1, 32),), jnp.float32),
        "mixing_offset": jnp.clip(jax.random.uniform(splits[12], (2 * GROUPS * N,), jnp.float32, -0.5, 0.5) * levels(splits[12], (2 * GROUPS * N,), ((0, 32),), -0.4, 0.0), -0.5, 0.5),
        "step_offset": jnp.clip(-4.0 + 4.0 * jax.random.uniform(splits[13], (HEADS,), jnp.float32) ** levels(splits[13], (HEADS,), ((0, 32),), -0.2, 0.2), -4.0, 0.0),
        "decay_log": jnp.clip(-2.0 + 3.5 * jax.random.uniform(splits[14], (HEADS,), jnp.float32) ** levels(splits[14], (HEADS,), ((0, 32),), -0.2, 0.2), -2.0, 1.5),
        "skip_gain": jnp.clip(0.5 + 1.0 * jax.random.uniform(splits[15], (HEADS,), jnp.float32) ** levels(splits[15], (HEADS,), ((0, 32),), -0.2, 0.2), 0.5, 1.5),
        "output_gain": jnp.clip(1.0 + 0.1 * jax.random.normal(splits[16], (HEADS * P_SIZE,), jnp.float32), 0.5, 1.5),
        "output_weight": noise(splits[17], (HEADS * P_SIZE, D), (HEADS * P_SIZE) ** -0.5, 0.0625, ((0, 32),)),
    }


def causal_conv(previous, current, kernel, shift_bias):
    window = jnp.concatenate([jnp.moveaxis(previous, 1, 0), current], axis=0)
    length = current.shape[0]
    summed = jnp.zeros_like(current)
    for tap_index in range(kernel.shape[0]):
        summed = summed + kernel[tap_index] * window[tap_index:tap_index + length]
    return jax.nn.silu(summed + shift_bias)

def reference(tokens, parents, recurrent_state, value_history, mixing_history, input_gain, gate_value_weight, mixing_weight, step_weight, value_kernel, value_offset, mixing_kernel, mixing_offset, step_offset, decay_log, skip_gain, output_gain, output_weight):
    channels = HEADS * P_SIZE
    heads_group = HEADS // GROUPS
    flat_tokens = tokens.astype(jnp.float32).reshape(STEPS * PARTICLES, D)
    normed = (flat_tokens * lax.rsqrt(lax.optimization_barrier(jnp.mean(flat_tokens * flat_tokens, axis=-1, keepdims=True)) + 1e-05) * input_gain).astype(jnp.bfloat16)
    gate_value = jnp.dot(normed, gate_value_weight.reshape(D, 2 * channels), preferred_element_type=jnp.float32).reshape(STEPS, PARTICLES, 2, channels)
    mixing_raw = jnp.dot(normed, mixing_weight, preferred_element_type=jnp.float32).reshape(STEPS, PARTICLES, 2 * GROUPS * N)
    step_raw = jnp.dot(normed, step_weight, preferred_element_type=jnp.float32).reshape(STEPS, PARTICLES, HEADS)
    value_prev = jnp.take(value_history, parents, axis=0)
    mixing_prev = jnp.take(mixing_history, parents, axis=0)
    value_act = causal_conv(value_prev, gate_value[:, :, 1], value_kernel, value_offset).reshape(STEPS, PARTICLES, HEADS, P_SIZE)
    mixing_act = causal_conv(mixing_prev, mixing_raw, mixing_kernel, mixing_offset)
    step_size = jax.nn.softplus(step_raw + step_offset)
    decay = jnp.exp(-step_size * jnp.exp(decay_log))

    def per_group(group_index):
        first_head = group_index * heads_group
        start_state = jnp.take(lax.dynamic_slice_in_dim(recurrent_state, first_head, heads_group, 1), parents, axis=0)
        input_mix = lax.dynamic_slice_in_dim(mixing_act, group_index * N, N, 2)
        output_mix = lax.dynamic_slice_in_dim(mixing_act, (GROUPS + group_index) * N, N, 2)
        values = lax.dynamic_slice_in_dim(value_act, first_head, heads_group, 2)
        sizes = lax.dynamic_slice_in_dim(step_size, first_head, heads_group, 2)
        decays = lax.dynamic_slice_in_dim(decay, first_head, heads_group, 2)
        skips = lax.dynamic_slice_in_dim(skip_gain, first_head, heads_group, 0)

        def advance(state_now, inputs):
            value_now, input_now, output_now, size_now, decay_now = inputs
            state_now = decay_now[:, :, None, None] * state_now + (size_now[:, :, None] * value_now)[..., None] * input_now[:, None, None, :]
            read_out = jnp.einsum('bhpn,bn->bhp', state_now, output_now, precision=lax.Precision.HIGHEST)
            return (state_now, read_out + skips[:, None] * value_now)
        unused_state, reads = lax.scan(advance, start_state, (values, input_mix, output_mix, sizes, decays))
        return reads
    reads = lax.map(per_group, jnp.arange(GROUPS, dtype=jnp.int32))
    read_all = jnp.moveaxis(reads, 0, 2).reshape(STEPS, PARTICLES, GROUPS, heads_group * P_SIZE)
    gated = read_all * jax.nn.silu(gate_value[:, :, 0].reshape(STEPS, PARTICLES, GROUPS, heads_group * P_SIZE))
    square_mean = lax.optimization_barrier(jnp.sum(gated * gated, axis=-1, keepdims=True)) / (heads_group * P_SIZE)
    scaled = ((gated * lax.rsqrt(square_mean + 1e-05)).reshape(STEPS * PARTICLES, channels) * output_gain).astype(jnp.bfloat16)
    mixed = jnp.dot(scaled, output_weight, preferred_element_type=jnp.float32).astype(jnp.bfloat16)
    return mixed.reshape(STEPS, PARTICLES, D)
```

```python
import jax
import jax.numpy as jnp
from jax import lax
from jax.sharding import PartitionSpec as P

STEPS = 24
LP = 16
ROWS = STEPS * LP
GROUPS = 4
LANES = 256
F32 = jnp.float32
BF16 = jnp.bfloat16


def silu(v):
    return v / (1.0 + jnp.exp(-v))


def conv_rows(window, kernel, bias):
    total = bias
    for k in range(4):
        total = total + kernel[k : k + 1] * window[k * LP : k * LP + ROWS]
    return silu(total)


def picked(hot, hist):
    return [jnp.dot(hot, hist[j], preferred_element_type=F32) for j in range(3)]


def body(
    tokens,
    parents,
    state,
    vhist,
    mhist,
    gain,
    gvw,
    mw,
    sw,
    vk,
    vo,
    mk,
    mo,
    so,
    dlog,
    skip,
    ogain,
    ow,
):
    d = lax.axis_index("dom")
    g = lax.axis_index("head") // 8
    full = lax.all_gather(tokens.reshape(ROWS, LANES), "head", axis=1, tiled=True)
    fgain = lax.all_gather(gain.astype(BF16), "head", axis=0, tiled=True).astype(F32)
    xf = full.astype(F32)
    inv = lax.rsqrt(jnp.mean(xf * xf, axis=-1, keepdims=True) + 1e-5)
    normed = (xf * inv * fgain).astype(BF16)
    gate = jnp.dot(normed, gvw[:, 0, :], preferred_element_type=F32)
    value = jnp.dot(normed, gvw[:, 1, :], preferred_element_type=F32)
    mixing = jnp.dot(normed, mw, preferred_element_type=F32)
    step_in = jnp.dot(normed, sw, preferred_element_type=F32)

    own = lax.dynamic_slice_in_dim(parents, d * LP, LP)
    hot = (own[:, None] == jnp.arange(64)[None, :]).astype(BF16)
    vall = lax.all_gather(
        jnp.moveaxis(vhist, 1, 0).astype(BF16), "dom", axis=1, tiled=True
    )
    mall = lax.all_gather(
        jnp.moveaxis(mhist, 1, 0).astype(BF16), "dom", axis=1, tiled=True
    )
    vact = conv_rows(jnp.concatenate(picked(hot, vall) + [value], 0), vk, vo[None])
    mact = conv_rows(jnp.concatenate(picked(hot, mall) + [mixing], 0), mk, mo[None])
    mixall = lax.all_gather(mact.astype(BF16), "head", axis=1, tiled=True)
    b = lax.dynamic_slice_in_dim(mixall, g * 256, 256, 1)
    c = lax.dynamic_slice_in_dim(mixall, (GROUPS + g) * 256, 256, 1)
    call = lax.all_gather(c, "dom", axis=0, tiled=False)

    sb = state.astype(BF16).reshape(LP, LANES, 256)
    row_parent = jnp.tile(parents.reshape(4, 1, LP), (1, STEPS, 1)).reshape(4 * ROWS)
    lhs = call.reshape(4 * ROWS, 256)
    u = jnp.zeros((4 * ROWS, LANES), F32)
    for q in range(LP):
        mask = (row_parent == d * LP + q).astype(BF16)[:, None]
        u = u + lax.dot_general(
            lhs * mask, sb[q], (((1,), (1,)), ((), ())), preferred_element_type=F32
        )
    from_state = lax.psum_scatter(
        u.astype(BF16).reshape(4, ROWS, LANES), "dom", scatter_dimension=0, tiled=True
    )[0].astype(F32)

    step = jax.nn.softplus(step_in + so[None])
    logdecay = -step * jnp.exp(dlog)[None]
    run = logdecay
    for sh in (1, 2, 4, 8, 16):
        z = jnp.zeros((sh * LP, 4), F32)
        run = run + jnp.concatenate([z, run[: ROWS - sh * LP]], 0)
    gram = lax.dot_general(c, b, (((1,), (1,)), ((), ())), preferred_element_type=F32)
    ri = lax.broadcasted_iota(jnp.int32, (ROWS, ROWS), 0)
    ci = lax.broadcasted_iota(jnp.int32, (ROWS, ROWS), 1)
    keep = ((ri % LP) == (ci % LP)) & (ci <= ri)
    gated = []
    for h in range(4):
        col = slice(64 * h, 64 * h + 64)
        diff = jnp.where(keep, run[:, h : h + 1] - run[:, h][None, :], -1e30)
        m = (gram * jnp.exp(diff)).astype(BF16)
        sv = (vact[:, col] * step[:, h : h + 1]).astype(BF16)
        y = jnp.dot(m, sv, preferred_element_type=F32)
        y = y + jnp.exp(run[:, h : h + 1]) * from_state[:, col]
        gated.append(y + skip[h] * vact[:, col])
    gated = jnp.concatenate(gated, 1) * silu(gate)
    sq = jnp.sum(gated * gated, axis=1)
    total = lax.psum(
        jnp.where(jnp.arange(GROUPS)[:, None] == g, sq[None, :], 0.0), "head"
    )
    total = jnp.sum(jnp.where(jnp.arange(GROUPS)[:, None] == g, total, 0.0), axis=0)
    inv2 = lax.rsqrt(total / 2048.0 + 1e-5)[:, None]
    scaled = (gated * inv2 * ogain[None]).astype(BF16)
    terms = jnp.dot(scaled, ow, preferred_element_type=F32).astype(BF16)
    out = lax.psum_scatter(terms, "head", scatter_dimension=1, tiled=True)
    return out.reshape(STEPS, LP, LANES)


def solution(mesh):
    return jax.shard_map(
        body,
        mesh=mesh,
        in_specs=(
            P(None, "dom", "head"),
            P(),
            P("dom", "head", None, None),
            P("dom", None, "head"),
            P("dom", None, "head"),
            P("head"),
            P(None, None, "head"),
            P(None, "head"),
            P(None, "head"),
            P(None, "head"),
            P("head"),
            P(None, "head"),
            P("head"),
            P("head"),
            P("head"),
            P("head"),
            P("head"),
            P("head", None),
        ),
        out_specs=P(None, "dom", "head"),
        check_vma=False,
    )
```

```python
import jax
import jax.numpy as jnp
from jax import lax
from jax.experimental import pallas as pl
from jax.experimental.pallas import tpu as pltpu
from jax.sharding import PartitionSpec as P

STEPS = 24
LP = 16
ROWS = STEPS * LP
HALF = ROWS // 2
TROWS = ROWS + 16
THALF = 208
LANES = 256
F32 = jnp.float32
BF16 = jnp.bfloat16
MESH = pl.DeviceIdType.MESH
NT = (((1,), (1,)), ((), ()))


def silu(v):
    return v / (1.0 + jnp.exp(-v))


def rel(j):
    return j + j // 2 - 2 * (j // 3)


def rcopy(src, dst, ssem, rsem, dev):
    return pltpu.make_async_remote_copy(
        src_ref=src,
        dst_ref=dst,
        send_sem=ssem,
        recv_sem=rsem,
        device_id=dev,
        device_id_type=MESH,
    )


def kernel(
    x_ref,
    pack,
    hist,
    hsel,
    par,
    step_t,
    v_hbm,
    mix_hbm,
    out_hbm,
    st_hbm,
    out_ref,
    tok,
    vraw,
    w,
    ms,
    wout,
    st,
    sbf,
    acc,
    accm,
    ss,
    hall,
    mixsend,
    mixrecv,
    bmat,
    cmat,
    cre,
    usend,
    urecv,
    uown,
    sv4,
    m4,
    gated,
    sqs,
    scaled,
    sbuf,
    rbuf,
    hsend,
    hrecv,
    fsend,
    frecv,
    rsum,
    load_sem,
    a_send,
    a_recv,
    as_send,
    as_recv,
    h_send,
    h_recv,
    m_send,
    m_recv,
    c_send,
    c_recv,
    u_send,
    u_recv,
    q_send,
    q_recv,
    r_send,
    r_recv,
    rs_send,
    rs_recv,
):
    d = lax.axis_index("dom")
    me = lax.axis_index("head")
    c = me % 2
    y = (me // 2) % 4
    z = me // 8
    s1 = 8 - 6 * c
    s2 = 2 + 6 * c
    p1 = z * (1 - c) + y * c
    p2 = y * (1 - c) + z * c
    sib = me + 1 - 2 * c

    def head(a, b):
        return {"head": a * s1 + b * s2 + c}

    def slot_own(i, k):
        return ((p1 + rel(i)) % 4) * s1 + ((p2 + rel(k)) % 4) * s2 + c

    def slot_sib(i, k):
        return ((p2 + rel(i)) % 4) * s2 + ((p1 + rel(k)) % 4) * s1 + 1 - c

    next1, prev1 = head((p1 + 1) % 4, p2), head((p1 + 3) % 4, p2)
    next2, prev2 = head(p1, (p2 + 1) % 4), head(p1, (p2 + 3) % 4)
    sibling = {"head": sib}

    def dom(o):
        return {"dom": (d + o) % 4}

    loads = []
    for i in range(8):
        rows = pl.ds(i * 4096, 4096)
        loads.append(
            pltpu.make_async_copy(v_hbm.at[rows], vraw.at[rows], load_sem.at[i])
        )
    loads.append(
        pltpu.make_async_copy(mix_hbm, ms.at[pl.ds(0, 64)], load_sem.at[8])
    )
    loads.append(pltpu.make_async_copy(st_hbm, st, load_sem.at[9]))
    loads.append(pltpu.make_async_copy(out_hbm, wout, load_sem.at[10]))
    for load in loads:
        load.start()

    barrier = pltpu.get_barrier_semaphore()

    @pl.loop(1, 32)
    def _(o):
        pl.semaphore_signal(
            barrier, inc=1, device_id={"head": (me + o) % 32}, device_id_type=MESH
        )

    for o in (1, 2, 3):
        pl.semaphore_signal(barrier, inc=1, device_id=dom(o), device_id_type=MESH)

    tok[me, 0:ROWS] = x_ref[...]
    tok[me, ROWS:TROWS] = jnp.broadcast_to(pack[7:8, :], (16, LANES)).astype(BF16)
    acc[...] = jnp.zeros_like(acc)
    accm[...] = jnp.zeros_like(accm)
    ss[...] = jnp.zeros_like(ss)
    ms[64:80, :] = step_t[...]
    ms[80:128, :] = jnp.zeros((48, 8192), BF16)
    hall[d] = hist[...]
    pl.semaphore_wait(barrier, 34)

    def ring(grp, idx, recv):
        k = (2, 1, 3, 3)[idx] if recv else (0, 0, 2, 1)[idx]
        slot = slot_own(k, 0) if grp == 4 else slot_own(grp, k)
        rows = (pl.ds(0, TROWS), pl.ds(0, TROWS), pl.ds(0, THALF), pl.ds(THALF, TROWS - THALF))[idx]
        to = (next1, prev1) if grp == 4 else (next2, prev2)
        ref = tok.at[slot, rows]
        return rcopy(ref, ref, a_send.at[grp, idx], a_recv.at[grp, idx], to[idx % 2])

    def to_sib(i, k, recv=False):
        slot = slot_sib(i, k) if recv else slot_own(i, k)
        ref = tok.at[slot]
        return rcopy(ref, ref, as_send.at[i * 4 + k], as_recv.at[i * 4 + k], sibling)

    ring(4, 0, False).start()
    ring(4, 1, False).start()
    ring(0, 0, False).start()
    ring(0, 1, False).start()
    to_sib(0, 0).start()

    hcopies = [
        rcopy(hall.at[d], hall.at[d], h_send.at[o - 1], h_recv.at[o - 1], dom(o))
        for o in (1, 2, 3)
    ]
    for copy in hcopies:
        copy.start()

    ri = lax.broadcasted_iota(jnp.int32, (256, 256), 0)
    ci = lax.broadcasted_iota(jnp.int32, (256, 256), 1)
    perm = (ci == 4 * (ri % 64) + ri // 64).astype(F32).astype(BF16)

    def split(b, _):
        v0 = pl.multiple_of(b * 512, 512)
        pair = jnp.concatenate(
            [vraw[pl.ds(v0, 256), :], vraw[pl.ds(v0 + 256, 256), :]], axis=1
        )
        res = jnp.dot(perm, pair, preferred_element_type=F32).astype(BF16)
        k0 = pl.multiple_of(b * 128, 128)
        for n in range(2):
            for j in range(2):
                for r in range(2):
                    m = 64 * (2 * j + r)
                    lane = 256 * r + 128 * j
                    w[pl.ds(k0 + 64 * n, 64), lane : lane + 128] = res[
                        m : m + 64, 128 * n : 128 * n + 128
                    ]
        return 0

    for i in range(4):
        loads[i].wait()
    lax.fori_loop(0, 32, split, 0)

    for idx, k in ((0, 2), (1, 1)):
        ring(4, idx, True).wait_recv()
        ring(4, 2 + idx, False).start()
        ring(k, 0, False).start()
        ring(k, 1, False).start()
        to_sib(k, 0).start()
    for i in range(4, 8):
        loads[i].wait()
    lax.fori_loop(32, 64, split, 0)
    for idx, k in ((0, 2), (1, 1)):
        ring(0, idx, True).wait_recv()
        ring(0, 2 + idx, False).start()
        to_sib(0, k).start()
    ring(4, 2, True).wait_recv()
    ring(4, 3, True).wait_recv()
    ring(3, 0, False).start()
    ring(3, 1, False).start()
    to_sib(3, 0).start()

    loads[8].wait()

    def project(slot):
        xf = tok[slot, 0:ROWS].astype(F32)
        grow = tok[slot, ROWS:TROWS].astype(F32)[0:1]
        sq = xf * xf
        ss[...] += sq[:, 0:128] + sq[:, 128:256]
        xg = (xf * grow).astype(BF16)
        k0 = pl.multiple_of(slot * 256, 256)
        acc[...] += jnp.dot(xg, w[pl.ds(k0, 256), :], preferred_element_type=F32)
        accm[...] += lax.dot_general(
            xg, ms[:, pl.ds(k0, 256)], NT, preferred_element_type=F32
        )

    def batch(count, which):
        def one(b, _):
            i, k = which(b // 2)
            side = b % 2

            @pl.when(side == 1)
            def _():
                to_sib(i, k, True).wait_recv()

            project(slot_own(i, k) * (1 - side) + slot_sib(i, k) * side)
            return 0

        lax.fori_loop(0, 2 * count, one, 0)

    loads[9].wait()

    def cast(q, _):
        sbf[:, pl.ds(pl.multiple_of(q * 256, 256), 256)] = st[q].astype(BF16)
        return 0

    lax.fori_loop(0, LP, cast, 0)
    batch(4, lambda b: (b, 0))
    for i in (1, 2):
        for idx, k in ((0, 2), (1, 1)):
            ring(i, idx, True).wait_recv()
            ring(i, 2 + idx, False).start()
            to_sib(i, k).start()
    ring(0, 2, True).wait_recv()
    ring(0, 3, True).wait_recv()
    to_sib(0, 3).start()
    batch(3, lambda b: (0, b + 1))
    for idx, k in ((0, 2), (1, 1)):
        ring(3, idx, True).wait_recv()
        ring(3, 2 + idx, False).start()
        to_sib(3, k).start()
    for i in (1, 2):
        ring(i, 2, True).wait_recv()
        ring(i, 3, True).wait_recv()
        to_sib(i, 3).start()
    batch(6, lambda b: (1 + b // 3, 1 + b % 3))
    batch(2, lambda b: (3, 1 + b))
    ring(3, 2, True).wait_recv()
    ring(3, 3, True).wait_recv()
    to_sib(3, 3).start()
    batch(1, lambda b: (3 + b, 3))

    inv = lax.rsqrt(jnp.sum(ss[...], axis=1, keepdims=True) / 8192.0 + 1e-5)

    for copy in hcopies:
        copy.wait()
    hprev = jnp.dot(
        hsel[...], hall[...].reshape(192, 384), preferred_element_type=F32
    )
    mtile = accm[...] * inv

    def conv(window, k0, bias, width):
        total = pack[bias : bias + 1, 0:width]
        for k in range(4):
            total = total + pack[k0 + k : k0 + k + 1, 0:width] * window[
                k * LP : k * LP + ROWS
            ]
        return silu(total)

    mact = conv(jnp.concatenate([hprev[:, 256:384], mtile], 0), 8, 12, 128)
    low = lax.broadcasted_iota(jnp.int32, (HALF, 128), 1) < 64
    mixsend[...] = jnp.where(
        low, mact[0:HALF], pltpu.roll(mact[HALF:ROWS], 64, 1)
    ).astype(BF16)
    first = ((me % 16) // 4) * 8
    place = (me // 16) * 4 + me % 4

    def mix_copy(n):
        return rcopy(
            mixsend, mixrecv.at[place], m_send.at[n], m_recv.at[place], {"head": first + n}
        )

    @pl.loop(0, 8)
    def _(n):
        @pl.when(first + n != me)
        def _():
            mix_copy(n).start()

        @pl.when(first + n == me)
        def _():
            pltpu.make_async_copy(mixsend, mixrecv.at[place], m_recv.at[place]).start()

    value = acc[:, 256:512] * inv
    vact = conv(jnp.concatenate([hprev[:, 0:256], value], 0), 0, 4, 256)
    gact = silu(acc[:, 0:256] * inv)
    step = mtile + pack[13:14, 0:128]
    step = jnp.maximum(step, 0.0) + jnp.log1p(jnp.exp(-jnp.abs(step)))
    run = -step * pack[14:15, 0:128]
    for sh in (1, 2, 4, 8, 16):
        z0 = jnp.zeros((sh * LP, 128), F32)
        run = run + jnp.concatenate([z0, run[: ROWS - sh * LP]], 0)
    run_t = run.T
    lane = lax.broadcasted_iota(jnp.int32, (ROWS, LANES), 1)

    def spread(t):
        out = jnp.broadcast_to(t[:, 67:68], (ROWS, LANES))
        for h in (2, 1, 0):
            out = jnp.where(lane < 64 * h + 64, t[:, 64 + h : 65 + h], out)
        return out

    sv = vact * spread(step)
    for h in range(4):
        inside = (lane >= 64 * h) & (lane < 64 * h + 64)
        sv4[h * ROWS : (h + 1) * ROWS, :] = jnp.where(inside, sv, 0.0).astype(BF16)

    @pl.loop(0, 8)
    def _(n):
        rcopy(mixsend, mixrecv.at[n], m_send.at[n], m_recv.at[n], sibling).wait_recv()

    def assemble(first_slot, dst):
        for t in range(2):
            a = mixrecv[first_slot + 2 * t].astype(F32)
            b = mixrecv[first_slot + 2 * t + 1].astype(F32)
            dst[0:HALF, 128 * t : 128 * t + 128] = jnp.where(
                low, a, pltpu.roll(b, 64, 1)
            ).astype(BF16)
            dst[HALF:ROWS, 128 * t : 128 * t + 128] = jnp.where(
                low, pltpu.roll(a, 64, 1), b
            ).astype(BF16)

    assemble(4, cmat)
    ccopies = [
        rcopy(cmat, cre.at[o - 1], c_send.at[o - 1], c_recv.at[o - 1], dom(o))
        for o in (1, 2, 3)
    ]
    for copy in ccopies:
        copy.start()
    assemble(0, bmat)

    gram = lax.dot_general(cmat[...], bmat[...], NT, preferred_element_type=F32)
    gi = lax.broadcasted_iota(jnp.int32, (ROWS, ROWS), 0)
    gj = lax.broadcasted_iota(jnp.int32, (ROWS, ROWS), 1)
    keep = ((gi % LP) == (gj % LP)) & (gj <= gi)
    for h in range(4):
        diff = jnp.where(keep, run[:, 64 + h : 65 + h] - run_t[64 + h : 65 + h, :], -1e30)
        m4[:, h * ROWS : (h + 1) * ROWS] = (gram * jnp.exp(diff)).astype(BF16)
    inner = jnp.dot(m4[...], sv4[...], preferred_element_type=F32)

    def reads(cref, e):
        def part(n, u):
            cval = cref[...].reshape(STEPS, LP, LANES)
            mine = par[pl.ds(pl.multiple_of(e * LP, LP), LP), :]
            lhs = []
            for t in range(4):
                q = (d * LP + n * 4 + t).astype(F32)
                mask = jnp.where(mine == q, 1.0, 0.0).astype(BF16)
                lhs.append((cval * mask[None]).reshape(ROWS, LANES))
            return u + lax.dot_general(
                jnp.concatenate(lhs, 1),
                sbf[:, pl.ds(pl.multiple_of(n * 1024, 1024), 1024)],
                NT,
                preferred_element_type=F32,
            )

        return lax.fori_loop(0, 4, part, jnp.zeros((ROWS, LANES), F32))

    ucopies = []
    for o in (1, 3, 2):
        ccopies[o - 1].wait_recv()
        usend[o - 1] = reads(cre.at[o - 1], (d + 4 - o) % 4).astype(BF16)
        ucopies.append(
            rcopy(usend.at[o - 1], urecv.at[o - 1], u_send.at[o - 1], u_recv.at[o - 1], dom(4 - o))
        )
        ucopies[-1].start()
    start_read = reads(cmat, d)
    for copy in ucopies:
        copy.wait_recv()
    for o in range(3):
        start_read = start_read + urecv[o].astype(F32)
    total = inner + jnp.exp(spread(run)) * start_read + pack[5:6, :] * vact
    total = total * gact
    sq = lax.dot_general(
        jnp.ones((8, LANES), F32),
        total * total,
        NT,
        preferred_element_type=F32,
        precision=lax.Precision.HIGHEST,
    )
    place8 = me % 8
    sqs[place8] = sq

    def sq_copy(o):
        at = (place8 + o) % 8
        return rcopy(
            sqs.at[place8], sqs.at[place8], q_send.at[o - 1], q_recv.at[o - 1], {"head": z * 8 + at}
        )

    for o in range(1, 8):
        sq_copy(o).start()
    for o in range(1, 8):
        at = (place8 + 8 - o) % 8
        rcopy(sqs.at[at], sqs.at[at], q_send.at[o - 1], q_recv.at[o - 1], sibling).wait_recv()
    tsq = sqs[0]
    for o in range(1, 8):
        tsq = tsq + sqs[o]
    inv2 = lax.rsqrt(tsq.T[:, 0:1] / 2048.0 + 1e-5)
    scaled[...] = (total * inv2 * pack[6:7, :]).astype(BF16)

    loads[10].wait()

    def terms(slot):
        return jnp.dot(
            scaled[...],
            wout[:, pl.ds(pl.multiple_of(slot * 256, 256), 256)],
            preferred_element_type=F32,
        )

    def sib_terms(n):
        return rcopy(sbuf.at[n], rbuf.at[n], rs_send.at[n], rs_recv.at[n], sibling)

    @pl.loop(0, 16)
    def _(t):
        n = (3 - t % 4) * 4 + 3 - t // 4
        sbuf[n] = terms(slot_sib(n // 4, n % 4)).astype(BF16)
        sib_terms(n).start()

    def mine(i, k):
        sib_terms(i * 4 + k).wait_recv()
        return terms(slot_own(i, k)) + rbuf[i * 4 + k].astype(F32)

    def half_copy(i, top, to):
        rows = pl.ds(0 if top else HALF, HALF)
        n = 0 if top else 1
        return rcopy(hsend.at[i, rows], hrecv.at[i, rows], r_send.at[i, n], r_recv.at[i, n], to)

    def full_copy(i, n, to):
        return rcopy(
            fsend.at[2 * i + n], frecv.at[2 * i + n], r_send.at[i, 2 + n], r_recv.at[i, 2 + n], to
        )

    @pl.loop(0, 4)
    def _(t):
        i = 3 - t
        hsend[i] = mine(i, 3).astype(BF16)
        half_copy(i, True, next2).start()
        half_copy(i, False, prev2).start()

    @pl.loop(0, 4)
    def _(t):
        i = 3 - t
        a = mine(i, 1)
        half_copy(i, True, next2).wait_recv()
        fsend[2 * i, 0:HALF] = (a[0:HALF] + hrecv[i, 0:HALF].astype(F32)).astype(BF16)
        fsend[2 * i, HALF:ROWS] = a[HALF:ROWS].astype(BF16)
        full_copy(i, 0, next2).start()
        b = mine(i, 2)
        half_copy(i, False, prev2).wait_recv()
        fsend[2 * i + 1, 0:HALF] = b[0:HALF].astype(BF16)
        fsend[2 * i + 1, HALF:ROWS] = (
            b[HALF:ROWS] + hrecv[i, HALF:ROWS].astype(F32)
        ).astype(BF16)
        full_copy(i, 1, prev2).start()

    @pl.loop(0, 4)
    def _(t):
        i = 3 - t
        a = mine(i, 0)
        full_copy(i, 0, next2).wait_recv()
        full_copy(i, 1, prev2).wait_recv()
        a = a + frecv[2 * i].astype(F32) + frecv[2 * i + 1].astype(F32)
        rsum[i] = a

        @pl.when(i == 3)
        def _():
            hsend[4] = a.astype(BF16)
            half_copy(4, True, next1).start()
            half_copy(4, False, prev1).start()

    half_copy(4, True, next1).wait_recv()
    fsend[8, 0:HALF] = (rsum[1, 0:HALF] + hrecv[4, 0:HALF].astype(F32)).astype(BF16)
    fsend[8, HALF:ROWS] = rsum[1, HALF:ROWS].astype(BF16)
    full_copy(4, 0, next1).start()
    half_copy(4, False, prev1).wait_recv()
    fsend[9, 0:HALF] = rsum[2, 0:HALF].astype(BF16)
    fsend[9, HALF:ROWS] = (
        rsum[2, HALF:ROWS] + hrecv[4, HALF:ROWS].astype(F32)
    ).astype(BF16)
    full_copy(4, 1, prev1).start()
    full_copy(4, 0, next1).wait_recv()
    full_copy(4, 1, prev1).wait_recv()
    out_ref[...] = (rsum[0] + frecv[8].astype(F32) + frecv[9].astype(F32)).astype(BF16)

    for grp in range(5):
        for idx in range(4):
            ring(grp, idx, False).wait_send()

    @pl.loop(0, 16)
    def _(n):
        to_sib(n // 4, n % 4).wait_send()
        sib_terms(n).wait_send()

    @pl.loop(0, 8)
    def _(n):
        @pl.when(first + n != me)
        def _():
            mix_copy(n).wait_send()

    for copy in ccopies + ucopies:
        copy.wait_send()
    for o in range(1, 8):
        sq_copy(o).wait_send()
    for i in range(5):
        nxt, prv = (next1, prev1) if i == 4 else (next2, prev2)
        half_copy(i, True, nxt).wait_send()
        half_copy(i, False, prv).wait_send()
        full_copy(i, 0, nxt).wait_send()
        full_copy(i, 1, prv).wait_send()


def body(
    tokens,
    parents,
    state,
    vhist,
    mhist,
    gain,
    gvw,
    mw,
    sw,
    vk,
    vo,
    mk,
    mo,
    so,
    dlog,
    skip,
    ogain,
    ow,
):
    d = lax.axis_index("dom")

    def wide(a, at=0):
        a = a.reshape(-1, a.shape[-1])
        return jnp.pad(a, ((0, 0), (at, 256 - at - a.shape[-1])))

    pack = jnp.concatenate(
        [
            vk,
            wide(vo),
            jnp.repeat(skip, 64)[None],
            wide(ogain),
            wide(gain),
            wide(mk),
            wide(mo),
            wide(so, 64),
            wide(jnp.exp(dlog), 64),
            jnp.zeros((1, 256), F32),
        ],
        0,
    )
    hist = jnp.concatenate(
        [
            jnp.moveaxis(vhist, 1, 0),
            jnp.pad(jnp.moveaxis(mhist, 1, 0), ((0, 0), (0, 0), (0, 64))),
        ],
        2,
    )
    hist = hist.astype(BF16).reshape(48, 384)
    own = lax.dynamic_slice_in_dim(parents, d * LP, LP)
    a = jnp.arange(48)[:, None]
    b = jnp.arange(192)[None, :]
    hsel = (
        (a // LP == (b // LP) % 3)
        & (jnp.tile(own, 3)[:, None] == (b // 48) * LP + b % LP)
    ).astype(BF16)
    par = jnp.broadcast_to(parents.astype(F32)[:, None], (64, 256))
    step_t = jnp.pad(sw.T, ((0, 12), (0, 0)))
    v = gvw.reshape(8192, 2, 2, 128).transpose(0, 2, 1, 3).reshape(32768, 128)

    vmem = pl.BlockSpec(memory_space=pltpu.VMEM)
    hbm = pl.BlockSpec(memory_space=pl.ANY)
    dma = pltpu.SemaphoreType.DMA
    big = (ROWS, LANES)
    out = pl.pallas_call(
        kernel,
        out_shape=jax.ShapeDtypeStruct(big, BF16),
        in_specs=[vmem] * 6 + [hbm] * 4,
        out_specs=vmem,
        scratch_shapes=[
            pltpu.VMEM((32, TROWS, LANES), BF16),
            pltpu.VMEM((32768, 128), BF16),
            pltpu.VMEM((8192, 512), BF16),
            pltpu.VMEM((128, 8192), BF16),
            pltpu.VMEM((256, 8192), BF16),
            pltpu.VMEM((LP, 256, 256), F32),
            pltpu.VMEM((256, LP * 256), BF16),
            pltpu.VMEM((ROWS, 512), F32),
            pltpu.VMEM((ROWS, 128), F32),
            pltpu.VMEM((ROWS, 128), F32),
            pltpu.VMEM((4, 48, 384), BF16),
            pltpu.VMEM((HALF, 128), BF16),
            pltpu.VMEM((8, HALF, 128), BF16),
            pltpu.VMEM(big, BF16),
            pltpu.VMEM(big, BF16),
            pltpu.VMEM((3, *big), BF16),
            pltpu.VMEM((3, *big), BF16),
            pltpu.VMEM((3, *big), BF16),
            pltpu.VMEM((8, 128), F32),
            pltpu.VMEM((4 * ROWS, LANES), BF16),
            pltpu.VMEM((ROWS, 4 * ROWS), BF16),
            pltpu.VMEM((8, 128), F32),
            pltpu.VMEM((8, 8, ROWS), F32),
            pltpu.VMEM(big, BF16),
            pltpu.VMEM((16, *big), BF16),
            pltpu.VMEM((16, *big), BF16),
            pltpu.VMEM((5, *big), BF16),
            pltpu.VMEM((5, *big), BF16),
            pltpu.VMEM((10, *big), BF16),
            pltpu.VMEM((10, *big), BF16),
            pltpu.VMEM((4, *big), F32),
            dma((11,)),
            dma((5, 4)),
            dma((5, 4)),
            dma((16,)),
            dma((16,)),
            dma((3,)),
            dma((3,)),
            dma((8,)),
            dma((8,)),
            dma((3,)),
            dma((3,)),
            dma((3,)),
            dma((3,)),
            dma((7,)),
            dma((7,)),
            dma((5, 4)),
            dma((5, 4)),
            dma((16,)),
            dma((16,)),
        ],
        compiler_params=pltpu.CompilerParams(
            collective_id=0,
            has_side_effects=True,
            vmem_limit_bytes=63 * 1024 * 1024,
        ),
    )(
        tokens.reshape(ROWS, LANES),
        pack,
        hist,
        hsel,
        par,
        step_t,
        v,
        mw.T,
        ow,
        state.reshape(LP, 256, 256),
    )
    return out.reshape(STEPS, LP, LANES)


def solution(mesh):
    return jax.shard_map(
        body,
        mesh=mesh,
        in_specs=(
            P(None, "dom", "head"),
            P(),
            P("dom", "head", None, None),
            P("dom", None, "head"),
            P("dom", None, "head"),
            P("head"),
            P(None, None, "head"),
            P(None, "head"),
            P(None, "head"),
            P(None, "head"),
            P("head"),
            P(None, "head"),
            P("head"),
            P("head"),
            P("head"),
            P("head"),
            P("head"),
            P("head", None),
        ),
        out_specs=P(None, "dom", "head"),
        check_vma=False,
    )
```

```python
import jax
import jax.numpy as jnp
from jax import lax
from jax.experimental import pallas as pl
from jax.experimental.pallas import tpu as pltpu
from jax.sharding import PartitionSpec as P

STEPS = 24
LP = 16
ROWS = STEPS * LP
HALF = ROWS // 2
TROWS = ROWS + 16
THALF = 208
LANES = 256
F32 = jnp.float32
BF16 = jnp.bfloat16
MESH = pl.DeviceIdType.MESH
NT = (((1,), (1,)), ((), ()))


def silu(v):
    return v / (1.0 + jnp.exp(-v))


def rel(j):
    return j + j // 2 - 2 * (j // 3)


def rcopy(src, dst, ssem, rsem, dev):
    return pltpu.make_async_remote_copy(
        src_ref=src,
        dst_ref=dst,
        send_sem=ssem,
        recv_sem=rsem,
        device_id=dev,
        device_id_type=MESH,
    )


def kernel(
    x_hbm,
    parents_hbm,
    vh_hbm,
    mh_hbm,
    gain_hbm,
    vk_hbm,
    vo_hbm,
    mk_hbm,
    mo_hbm,
    so_hbm,
    dlog_hbm,
    skip_hbm,
    ogain_hbm,
    step_hbm,
    v_hbm,
    mix_hbm,
    out_hbm,
    st_hbm,
    out_ref,
    parents,
    vh,
    mh,
    gain,
    vk,
    vo,
    mk,
    mo,
    so,
    dlog,
    skip,
    ogain,
    step_w,
    par,
    tok,
    vraw,
    w,
    ms,
    wout,
    st,
    sbf,
    acc,
    accm,
    ss,
    hall,
    mixsend,
    mixrecv,
    bmat,
    call,
    ufar,
    ufarr,
    usend,
    urecv,
    sv4,
    m4,
    sqs,
    scaled,
    inv2s,
    sbuf,
    rbuf,
    hsend,
    hrecv,
    fsend,
    frecv,
    rsum,
    load_sem,
    small_sem,
    a_send,
    a_recv,
    as_send,
    as_recv,
    h_send,
    h_recv,
    m_send,
    m_recv,
    mf_send,
    c_send,
    c_recv,
    cs_send,
    cs_recv,
    u_send,
    u_recv,
    q_send,
    q_recv,
    r_send,
    r_recv,
    rs_send,
    rs_recv,
):
    d = lax.axis_index("dom")
    me = lax.axis_index("head")
    c = me % 2
    y = (me // 2) % 4
    z = me // 8
    s1 = 8 - 6 * c
    s2 = 2 + 6 * c
    p1 = z * (1 - c) + y * c
    p2 = y * (1 - c) + z * c
    sib = me + 1 - 2 * c

    def head(a, b):
        return {"head": a * s1 + b * s2 + c}

    def slot_own(i, k):
        return ((p1 + rel(i)) % 4) * s1 + ((p2 + rel(k)) % 4) * s2 + c

    def slot_sib(i, k):
        return ((p2 + rel(i)) % 4) * s2 + ((p1 + rel(k)) % 4) * s1 + 1 - c

    next1, prev1 = head((p1 + 1) % 4, p2), head((p1 + 3) % 4, p2)
    next2, prev2 = head(p1, (p2 + 1) % 4), head(p1, (p2 + 3) % 4)
    sibling = {"head": sib}

    def dom(o):
        return {"dom": (d + o) % 4}

    small = [
        pltpu.make_async_copy(src, dst, small_sem.at[n])
        for n, (src, dst) in enumerate(
            (
                (x_hbm, tok.at[me, pl.ds(0, ROWS)]),
                (gain_hbm, gain),
                (parents_hbm, parents),
                (vh_hbm, vh),
                (mh_hbm, mh),
                (vk_hbm, vk),
                (vo_hbm, vo),
                (mk_hbm, mk),
                (mo_hbm, mo),
                (so_hbm, so),
                (dlog_hbm, dlog),
                (skip_hbm, skip),
                (ogain_hbm, ogain),
                (step_hbm, step_w),
            )
        )
    ]
    for load in small:
        load.start()

    barrier = pltpu.get_barrier_semaphore()
    for dev in (next1, prev1, next2, prev2, sibling, dom(1), dom(2), dom(3)):
        pl.semaphore_signal(barrier, inc=1, device_id=dev, device_id_type=MESH)

    loads = []
    for i in range(8):
        rows = pl.ds(i * 4096, 4096)
        loads.append(
            pltpu.make_async_copy(v_hbm.at[rows], vraw.at[rows], load_sem.at[i])
        )
    loads.append(
        pltpu.make_async_copy(mix_hbm, ms.at[pl.ds(0, 64)], load_sem.at[8])
    )
    loads.append(pltpu.make_async_copy(st_hbm, st, load_sem.at[9]))
    loads.append(pltpu.make_async_copy(out_hbm, wout, load_sem.at[10]))
    for load in loads:
        load.start()
    for load in small:
        load.wait()
    tok[me, ROWS:TROWS] = jnp.broadcast_to(gain[...], (16, LANES)).astype(BF16)
    for n in range(3):
        rows = pl.ds(n * LP, LP)
        hall[d, rows, 0:256] = vh[rows, :].astype(BF16)
        hall[d, rows, 256:384] = jnp.concatenate(
            [mh[rows, :], jnp.zeros((LP, 64), F32)], 1
        ).astype(BF16)
    pl.semaphore_wait(barrier, 8)

    def ring(grp, idx, recv):
        k = (2, 1, 3, 3)[idx] if recv else (0, 0, 2, 1)[idx]
        slot = slot_own(k, 0) if grp == 4 else slot_own(grp, k)
        rows = (pl.ds(0, TROWS), pl.ds(0, TROWS), pl.ds(0, THALF), pl.ds(THALF, TROWS - THALF))[idx]
        to = (next1, prev1) if grp == 4 else (next2, prev2)
        ref = tok.at[slot, rows]
        return rcopy(ref, ref, a_send.at[grp, idx], a_recv.at[grp, idx], to[idx % 2])

    def to_sib(i, k, recv=False):
        slot = slot_sib(i, k) if recv else slot_own(i, k)
        ref = tok.at[slot]
        return rcopy(ref, ref, as_send.at[i * 4 + k], as_recv.at[i * 4 + k], sibling)

    ring(4, 0, False).start()
    ring(4, 1, False).start()
    ring(0, 0, False).start()
    ring(0, 1, False).start()
    to_sib(0, 0).start()

    hcopies = [
        rcopy(hall.at[d], hall.at[d], h_send.at[o - 1], h_recv.at[o - 1], dom(o))
        for o in (1, 2, 3)
    ]
    for copy in hcopies:
        copy.start()

    acc[...] = jnp.zeros_like(acc)
    accm[...] = jnp.zeros_like(accm)
    ss[...] = jnp.zeros_like(ss)
    ms[64:80, :] = jnp.concatenate(
        [step_w[...].astype(F32), jnp.zeros((12, 8192), F32)], 0
    ).astype(BF16)
    ms[80:128, :] = jnp.zeros((48, 8192), BF16)
    pi = lax.broadcasted_iota(jnp.int32, (64, 64), 0)
    pj = lax.broadcasted_iota(jnp.int32, (64, 64), 1)
    par[...] = jnp.broadcast_to(
        jnp.sum(jnp.where(pi == pj, parents[...].astype(F32), 0.0), 1, keepdims=True),
        (64, LANES),
    )

    ri = lax.broadcasted_iota(jnp.int32, (256, 256), 0)
    ci = lax.broadcasted_iota(jnp.int32, (256, 256), 1)
    perm = (ci == 4 * (ri % 64) + ri // 64).astype(F32).astype(BF16)

    def split(b, _):
        v0 = pl.multiple_of(b * 512, 512)
        pair = jnp.concatenate(
            [vraw[pl.ds(v0, 256), :], vraw[pl.ds(v0 + 256, 256), :]], axis=1
        )
        res = jnp.dot(perm, pair, preferred_element_type=F32).astype(BF16)
        k0 = pl.multiple_of(b * 128, 128)
        for n in range(2):
            for j in range(2):
                for r in range(2):
                    m = 64 * (2 * j + r)
                    lane = 256 * r + 128 * j
                    w[pl.ds(k0 + 64 * n, 64), lane : lane + 128] = res[
                        m : m + 64, 128 * n : 128 * n + 128
                    ]
        return 0

    for i in range(4):
        loads[i].wait()
    lax.fori_loop(0, 32, split, 0)

    for idx, k in ((0, 2), (1, 1)):
        ring(4, idx, True).wait_recv()
        ring(4, 2 + idx, False).start()
        ring(k, 0, False).start()
        ring(k, 1, False).start()
        to_sib(k, 0).start()
    for i in range(4, 8):
        loads[i].wait()
    lax.fori_loop(32, 64, split, 0)
    for idx, k in ((0, 2), (1, 1)):
        ring(0, idx, True).wait_recv()
        ring(0, 2 + idx, False).start()
        to_sib(0, k).start()
    ring(4, 2, True).wait_recv()
    ring(4, 3, True).wait_recv()
    ring(3, 0, False).start()
    ring(3, 1, False).start()
    to_sib(3, 0).start()

    loads[8].wait()

    def project(i, k):
        to_sib(i, k, True).wait_recv()
        lhs, wide_rhs, narrow_rhs = [], [], []
        part = ss[...]
        for slot in (slot_own(i, k), slot_sib(i, k)):
            xf = tok[slot, 0:ROWS].astype(F32)
            grow = tok[slot, ROWS:TROWS].astype(F32)[0:1]
            sq = xf * xf
            part = part + sq[:, 0:128] + sq[:, 128:256]
            lhs.append((xf * grow).astype(BF16))
            k0 = pl.multiple_of(slot * 256, 256)
            wide_rhs.append(w[pl.ds(k0, 256), :])
            narrow_rhs.append(ms[:, pl.ds(k0, 256)])
        ss[...] = part
        xg = jnp.concatenate(lhs, 1)
        acc[...] += jnp.dot(
            xg, jnp.concatenate(wide_rhs, 0), preferred_element_type=F32
        )
        accm[...] += lax.dot_general(
            xg, jnp.concatenate(narrow_rhs, 1), NT, preferred_element_type=F32
        )

    def batch(count, which):
        def one(b, _):
            project(*which(b))
            return 0

        lax.fori_loop(0, count, one, 0)

    def cast(q, _):
        sbf[:, pl.ds(pl.multiple_of(q * 256, 256), 256)] = st[q].astype(BF16)
        return 0

    def pass_on(i):
        for idx, k in ((0, 2), (1, 1)):
            ring(i, idx, True).wait_recv()
            ring(i, 2 + idx, False).start()
            to_sib(i, k).start()

    def far(i):
        ring(i, 2, True).wait_recv()
        ring(i, 3, True).wait_recv()
        to_sib(i, 3).start()

    batch(1, lambda b: (b, 0))
    pass_on(1)
    batch(1, lambda b: (b + 1, 0))
    pass_on(2)
    loads[9].wait()
    lax.fori_loop(0, LP, cast, 0)
    far(0)
    batch(2, lambda b: (2 + b, 0))
    pass_on(3)
    batch(3, lambda b: (0, b + 1))
    far(1)
    batch(2, lambda b: (1, b + 1))
    far(2)
    batch(3, lambda b: (1 + (b + 2) // 3, 3 * (1 - (b + 2) // 3) + b))
    batch(3, lambda b: (2 + (b + 1) // 2, 3 * (1 - (b + 1) // 2) + b))
    far(3)
    batch(1, lambda b: (3 + b, 3))

    inv = lax.rsqrt(jnp.sum(ss[...], axis=1, keepdims=True) / 8192.0 + 1e-5)

    for copy in hcopies:
        copy.wait()
    hi = lax.broadcasted_iota(jnp.int32, (LP, 192), 1)
    same = par[pl.ds(pl.multiple_of(d * LP, LP), LP), 0:192] == (
        (hi // 48) * LP + hi % LP
    ).astype(F32)
    hot = jnp.concatenate(
        [
            jnp.where(same & ((hi // LP) % 3 == n), 1.0, 0.0).astype(BF16)
            for n in range(3)
        ],
        0,
    )
    hprev = jnp.dot(hot, hall[...].reshape(192, 384), preferred_element_type=F32)
    mtile = accm[...] * inv

    def conv(window, taps, bias):
        total = bias
        for k in range(4):
            total = total + taps[k : k + 1] * window[k * LP : k * LP + ROWS]
        return silu(total)

    wide4 = jnp.zeros((4, 64), F32)
    mact = conv(
        jnp.concatenate([hprev[:, 256:384], mtile], 0),
        jnp.concatenate([mk[...], wide4], 1),
        jnp.concatenate([mo[...], wide4[0:1]], 1),
    )
    low = lax.broadcasted_iota(jnp.int32, (HALF, 128), 1) < 64
    mixsend[...] = jnp.where(
        low, mact[0:HALF], pltpu.roll(mact[HALF:ROWS], 64, 1)
    ).astype(BF16)
    first = ((me % 16) // 4) * 8 + c
    place = (me // 16) * 4 + me % 4

    def mix_copy(n):
        return rcopy(
            mixsend, mixrecv.at[place], m_send.at[n], m_recv.at[place], {"head": first + 2 * n}
        )

    @pl.loop(0, 4)
    def _(n):
        @pl.when(first + 2 * n != me)
        def _():
            mix_copy(n).start()

        @pl.when(first + 2 * n == me)
        def _():
            pltpu.make_async_copy(mixsend, mixrecv.at[place], m_recv.at[place]).start()

    def mix_pass(n):
        return rcopy(mixrecv.at[n], mixrecv.at[n], mf_send.at[n], m_recv.at[n], sibling)

    value = acc[:, 256:512] * inv
    vact = conv(jnp.concatenate([hprev[:, 0:256], value], 0), vk, vo[...])
    row = lax.broadcasted_iota(jnp.int32, (1, 128), 1)

    def heads_row(ref):
        out = jnp.zeros((1, 128), F32)
        for h in range(4):
            out = jnp.where(row == 64 + h, ref[0:1, h : h + 1], out)
        return out

    step = mtile + heads_row(so)
    step = jnp.maximum(step, 0.0) + jnp.log1p(jnp.exp(-jnp.abs(step)))
    run = -step * jnp.exp(heads_row(dlog))
    for sh in (1, 2, 4, 8, 16):
        z0 = jnp.zeros((sh * LP, 128), F32)
        run = run + jnp.concatenate([z0, run[: ROWS - sh * LP]], 0)
    run_t = run.T
    lane = lax.broadcasted_iota(jnp.int32, (ROWS, LANES), 1)

    def spread(t, at=64):
        out = jnp.broadcast_to(t[:, at + 3 : at + 4], (t.shape[0], LANES))
        for h in (2, 1, 0):
            out = jnp.where(
                lane[0 : t.shape[0]] < 64 * h + 64, t[:, at + h : at + h + 1], out
            )
        return out

    for n in (4, 6):
        mix_pass(n + c).wait_recv()
        mix_pass(n + c).start()
    for n in (4, 6):
        mix_pass(n + 1 - c).wait_recv()

    def assemble(first_slot, dst):
        for t in range(2):
            a = mixrecv[first_slot + 2 * t].astype(F32)
            b = mixrecv[first_slot + 2 * t + 1].astype(F32)
            dst[0:HALF, 128 * t : 128 * t + 128] = jnp.where(
                low, a, pltpu.roll(b, 64, 1)
            ).astype(BF16)
            dst[HALF:ROWS, 128 * t : 128 * t + 128] = jnp.where(
                low, pltpu.roll(a, 64, 1), b
            ).astype(BF16)

    cmat = call.at[d]
    assemble(4, cmat)
    x0 = pl.multiple_of(c * HALF, HALF)
    quarter = HALF // 2

    def c_copy(idx, recv):
        e = (d + ((3, 1, 2, 2)[idx] if recv else (0, 0, 3, 1)[idx])) % 4
        rows = (
            pl.ds(x0, HALF),
            pl.ds(x0, HALF),
            pl.ds(x0, quarter),
            pl.ds(x0 + quarter, quarter),
        )[idx]
        ref = call.at[e, rows]
        return rcopy(ref, ref, c_send.at[idx], c_recv.at[idx], dom((1, 3)[idx % 2]))

    def c_pass(o, recv):
        start = pl.multiple_of((1 - c) * HALF, HALF) if recv else x0
        ref = call.at[(d + o) % 4, pl.ds(start, HALF)]
        return rcopy(ref, ref, cs_send.at[o - 1], cs_recv.at[o - 1], sibling)

    c_copy(0, False).start()
    c_copy(1, False).start()
    for n in (0, 2):
        mix_pass(n + c).wait_recv()
        mix_pass(n + c).start()

    def reads(e):
        mine = par[pl.ds(pl.multiple_of(e * LP, LP), LP), :]

        def part(n, u):
            cval = call[e].reshape(STEPS, LP, LANES)
            lhs = []
            for t in range(4):
                q = (d * LP + n * 4 + t).astype(F32)
                mask = jnp.where(mine == q, 1.0, 0.0).astype(BF16)
                lhs.append((cval * mask[None]).reshape(ROWS, LANES))
            return u + lax.dot_general(
                jnp.concatenate(lhs, 1),
                sbf[:, pl.ds(pl.multiple_of(n * 1024, 1024), 1024)],
                NT,
                preferred_element_type=F32,
            )

        return lax.fori_loop(0, 4, part, jnp.zeros((ROWS, LANES), F32))

    start_read = reads(d)
    for idx, o in ((0, 3), (1, 1)):
        c_copy(idx, True).wait_recv()
        c_copy(2 + idx, False).start()
        c_pass(o, False).start()
    for n in (0, 2):
        mix_pass(n + 1 - c).wait_recv()
    assemble(0, bmat)
    gram = lax.dot_general(cmat[...], bmat[...], NT, preferred_element_type=F32)
    gact = silu(acc[:, 0:256] * inv)
    c_copy(2, True).wait_recv()
    c_copy(3, True).wait_recv()
    c_pass(2, False).start()
    c_pass(2, True).wait_recv()
    ufar[...] = reads((d + 2) % 4).astype(BF16)

    def u_half(top):
        rows = pl.ds(0 if top else HALF, HALF)
        n = 0 if top else 1
        return rcopy(
            ufar.at[rows], ufarr.at[rows], u_send.at[n], u_recv.at[n], dom(1 if top else 3)
        )

    def u_full(n):
        return rcopy(
            usend.at[n], urecv.at[n], u_send.at[2 + n], u_recv.at[2 + n], dom(1 + 2 * n)
        )

    u_half(True).start()
    u_half(False).start()
    c_pass(1, True).wait_recv()
    a = reads((d + 1) % 4).astype(BF16)
    u_half(True).wait_recv()
    usend[0, 0:HALF] = a[0:HALF] + ufarr[0:HALF]
    usend[0, HALF:ROWS] = a[HALF:ROWS]
    u_full(0).start()
    c_pass(3, True).wait_recv()
    a = reads((d + 3) % 4).astype(BF16)
    u_half(False).wait_recv()
    usend[1, 0:HALF] = a[0:HALF]
    usend[1, HALF:ROWS] = a[HALF:ROWS] + ufarr[HALF:ROWS]
    u_full(1).start()

    sv = vact * spread(step)
    for h in range(4):
        inside = (lane >= 64 * h) & (lane < 64 * h + 64)
        sv4[h * ROWS : (h + 1) * ROWS, :] = jnp.where(inside, sv, 0.0).astype(BF16)
    gi = lax.broadcasted_iota(jnp.int32, (ROWS, ROWS), 0)
    gj = lax.broadcasted_iota(jnp.int32, (ROWS, ROWS), 1)
    keep = ((gi % LP) == (gj % LP)) & (gj <= gi)
    for h in range(4):
        diff = jnp.where(keep, run[:, 64 + h : 65 + h] - run_t[64 + h : 65 + h, :], -1e30)
        m4[:, h * ROWS : (h + 1) * ROWS] = (gram * jnp.exp(diff)).astype(BF16)
    inner = jnp.dot(m4[...], sv4[...], preferred_element_type=F32)
    inner = inner + spread(skip[...], 0) * vact
    carry = spread(jnp.exp(run))
    u_full(0).wait_recv()
    u_full(1).wait_recv()
    start_read = start_read + urecv[0].astype(F32) + urecv[1].astype(F32)
    total = (inner + carry * start_read) * gact
    scaled[...] = (total * ogain[...]).astype(BF16)
    sq = lax.dot_general(
        jnp.ones((8, LANES), F32),
        total * total,
        NT,
        preferred_element_type=F32,
        precision=lax.Precision.HIGHEST,
    )
    place8 = me % 8
    sqs[place8] = sq

    def sq_copy(o):
        at = (place8 + o) % 8
        return rcopy(
            sqs.at[place8], sqs.at[place8], q_send.at[o - 1], q_recv.at[o - 1], {"head": z * 8 + at}
        )

    for o in range(1, 8):
        sq_copy(o).start()

    loads[10].wait()

    def terms(slot):
        return jnp.dot(
            scaled[...],
            wout[:, pl.ds(pl.multiple_of(slot * 256, 256), 256)],
            preferred_element_type=F32,
        )

    def sib_terms(n):
        return rcopy(sbuf.at[n], rbuf.at[n], rs_send.at[n], rs_recv.at[n], sibling)

    def give(i, k):
        n = i * 4 + k
        sbuf[n] = terms(slot_sib(i, k)).astype(BF16)
        sib_terms(n).start()

    @pl.loop(0, 4)
    def _(t):
        give(3 - t, 3)

    for o in range(1, 8):
        at = (place8 + 8 - o) % 8
        rcopy(sqs.at[at], sqs.at[at], q_send.at[o - 1], q_recv.at[o - 1], sibling).wait_recv()
    tsq = sqs[0]
    for o in range(1, 8):
        tsq = tsq + sqs[o]
    inv2 = lax.rsqrt(tsq.T[:, 0:1] / 2048.0 + 1e-5)
    inv2s[...] = jnp.broadcast_to(inv2, (ROWS, LANES))

    def mine(i, k):
        sib_terms(i * 4 + k).wait_recv()
        return (terms(slot_own(i, k)) + rbuf[i * 4 + k].astype(F32)) * inv2s[...]

    def half_copy(i, top, to):
        rows = pl.ds(0 if top else HALF, HALF)
        n = 0 if top else 1
        return rcopy(hsend.at[i, rows], hrecv.at[i, rows], r_send.at[i, n], r_recv.at[i, n], to)

    def full_copy(i, n, to):
        return rcopy(
            fsend.at[2 * i + n], frecv.at[2 * i + n], r_send.at[i, 2 + n], r_recv.at[i, 2 + n], to
        )

    @pl.loop(0, 4)
    def _(t):
        i = 3 - t
        give(i, 1)
        give(i, 2)
        hsend[i] = mine(i, 3).astype(BF16)
        half_copy(i, True, next2).start()
        half_copy(i, False, prev2).start()

    @pl.loop(0, 4)
    def _(t):
        i = 3 - t
        give(i, 0)
        a = mine(i, 1)
        half_copy(i, True, next2).wait_recv()
        fsend[2 * i, 0:HALF] = (a[0:HALF] + hrecv[i, 0:HALF].astype(F32)).astype(BF16)
        fsend[2 * i, HALF:ROWS] = a[HALF:ROWS].astype(BF16)
        full_copy(i, 0, next2).start()
        b = mine(i, 2)
        half_copy(i, False, prev2).wait_recv()
        fsend[2 * i + 1, 0:HALF] = b[0:HALF].astype(BF16)
        fsend[2 * i + 1, HALF:ROWS] = (
            b[HALF:ROWS] + hrecv[i, HALF:ROWS].astype(F32)
        ).astype(BF16)
        full_copy(i, 1, prev2).start()

    @pl.loop(0, 4)
    def _(t):
        i = 3 - t
        a = mine(i, 0)
        full_copy(i, 0, next2).wait_recv()
        full_copy(i, 1, prev2).wait_recv()
        a = a + frecv[2 * i].astype(F32) + frecv[2 * i + 1].astype(F32)
        rsum[i] = a

        @pl.when(i == 3)
        def _():
            hsend[4] = a.astype(BF16)
            half_copy(4, True, next1).start()
            half_copy(4, False, prev1).start()

    half_copy(4, True, next1).wait_recv()
    fsend[8, 0:HALF] = (rsum[1, 0:HALF] + hrecv[4, 0:HALF].astype(F32)).astype(BF16)
    fsend[8, HALF:ROWS] = rsum[1, HALF:ROWS].astype(BF16)
    full_copy(4, 0, next1).start()
    half_copy(4, False, prev1).wait_recv()
    fsend[9, 0:HALF] = rsum[2, 0:HALF].astype(BF16)
    fsend[9, HALF:ROWS] = (
        rsum[2, HALF:ROWS] + hrecv[4, HALF:ROWS].astype(F32)
    ).astype(BF16)
    full_copy(4, 1, prev1).start()
    full_copy(4, 0, next1).wait_recv()
    full_copy(4, 1, prev1).wait_recv()
    out_ref[...] = (rsum[0] + frecv[8].astype(F32) + frecv[9].astype(F32)).astype(BF16)

    for grp in range(5):
        for idx in range(4):
            ring(grp, idx, False).wait_send()

    @pl.loop(0, 16)
    def _(n):
        to_sib(n // 4, n % 4).wait_send()
        sib_terms(n).wait_send()

    @pl.loop(0, 4)
    def _(n):
        @pl.when(first + 2 * n != me)
        def _():
            mix_copy(n).wait_send()

        mix_pass(2 * n + c).wait_send()

    for idx in range(4):
        c_copy(idx, False).wait_send()
    for o in (1, 2, 3):
        c_pass(o, False).wait_send()
    for flag in (0, 1):
        u_half(flag == 0).wait_send()
        u_full(flag).wait_send()
    for o in range(1, 8):
        sq_copy(o).wait_send()
    for i in range(5):
        nxt, prv = (next1, prev1) if i == 4 else (next2, prev2)
        half_copy(i, True, nxt).wait_send()
        half_copy(i, False, prv).wait_send()
        full_copy(i, 0, nxt).wait_send()
        full_copy(i, 1, prv).wait_send()


def body(
    tokens,
    parents,
    state,
    vhist,
    mhist,
    gain,
    gvw,
    mw,
    sw,
    vk,
    vo,
    mk,
    mo,
    so,
    dlog,
    skip,
    ogain,
    ow,
):
    v = gvw.reshape(8192, 2, 2, 128).transpose(0, 2, 1, 3).reshape(32768, 128)

    vmem = pl.BlockSpec(memory_space=pltpu.VMEM)
    hbm = pl.BlockSpec(memory_space=pl.ANY)
    dma = pltpu.SemaphoreType.DMA
    big = (ROWS, LANES)
    out = pl.pallas_call(
        kernel,
        out_shape=jax.ShapeDtypeStruct(big, BF16),
        in_specs=[hbm] * 18,
        out_specs=vmem,
        scratch_shapes=[
            pltpu.VMEM((1, 64), jnp.int32),
            pltpu.VMEM((48, 256), F32),
            pltpu.VMEM((48, 64), F32),
            pltpu.VMEM((1, 256), F32),
            pltpu.VMEM((4, 256), F32),
            pltpu.VMEM((1, 256), F32),
            pltpu.VMEM((4, 64), F32),
            pltpu.VMEM((1, 64), F32),
            pltpu.VMEM((1, 4), F32),
            pltpu.VMEM((1, 4), F32),
            pltpu.VMEM((1, 4), F32),
            pltpu.VMEM((1, 256), F32),
            pltpu.VMEM((4, 8192), BF16),
            pltpu.VMEM((64, LANES), F32),
            pltpu.VMEM((32, TROWS, LANES), BF16),
            pltpu.VMEM((32768, 128), BF16),
            pltpu.VMEM((8192, 512), BF16),
            pltpu.VMEM((128, 8192), BF16),
            pltpu.VMEM((256, 8192), BF16),
            pltpu.VMEM((LP, 256, 256), F32),
            pltpu.VMEM((256, LP * 256), BF16),
            pltpu.VMEM((ROWS, 512), F32),
            pltpu.VMEM((ROWS, 128), F32),
            pltpu.VMEM((ROWS, 128), F32),
            pltpu.VMEM((4, 48, 384), BF16),
            pltpu.VMEM((HALF, 128), BF16),
            pltpu.VMEM((8, HALF, 128), BF16),
            pltpu.VMEM(big, BF16),
            pltpu.VMEM((4, *big), BF16),
            pltpu.VMEM(big, BF16),
            pltpu.VMEM(big, BF16),
            pltpu.VMEM((2, *big), BF16),
            pltpu.VMEM((2, *big), BF16),
            pltpu.VMEM((4 * ROWS, LANES), BF16),
            pltpu.VMEM((ROWS, 4 * ROWS), BF16),
            pltpu.VMEM((8, 8, ROWS), F32),
            pltpu.VMEM(big, BF16),
            pltpu.VMEM(big, F32),
            pltpu.VMEM((16, *big), BF16),
            pltpu.VMEM((16, *big), BF16),
            pltpu.VMEM((5, *big), BF16),
            pltpu.VMEM((5, *big), BF16),
            pltpu.VMEM((10, *big), BF16),
            pltpu.VMEM((10, *big), BF16),
            pltpu.VMEM((4, *big), F32),
            dma((11,)),
            dma((14,)),
            dma((5, 4)),
            dma((5, 4)),
            dma((16,)),
            dma((16,)),
            dma((3,)),
            dma((3,)),
            dma((4,)),
            dma((8,)),
            dma((8,)),
            dma((4,)),
            dma((4,)),
            dma((3,)),
            dma((3,)),
            dma((4,)),
            dma((4,)),
            dma((7,)),
            dma((7,)),
            dma((5, 4)),
            dma((5, 4)),
            dma((16,)),
            dma((16,)),
        ],
        compiler_params=pltpu.CompilerParams(
            collective_id=0,
            has_side_effects=True,
            vmem_limit_bytes=63 * 1024 * 1024,
        ),
    )(
        tokens.reshape(ROWS, LANES),
        parents.reshape(1, 64),
        vhist.transpose(1, 0, 2).reshape(48, LANES),
        mhist.transpose(1, 0, 2).reshape(48, 64),
        gain.reshape(1, LANES),
        vk,
        vo.reshape(1, LANES),
        mk,
        mo.reshape(1, 64),
        so.reshape(1, 4),
        dlog.reshape(1, 4),
        skip.reshape(1, 4),
        ogain.reshape(1, LANES),
        sw.T,
        v,
        mw.T,
        ow,
        state.reshape(LP, 256, 256),
    )
    return out.reshape(STEPS, LP, LANES)


def solution(mesh):
    return jax.shard_map(
        body,
        mesh=mesh,
        in_specs=(
            P(None, "dom", "head"),
            P(),
            P("dom", "head", None, None),
            P("dom", None, "head"),
            P("dom", None, "head"),
            P("head"),
            P(None, None, "head"),
            P(None, "head"),
            P(None, "head"),
            P(None, "head"),
            P("head"),
            P(None, "head"),
            P("head"),
            P("head"),
            P("head"),
            P("head"),
            P("head"),
            P("head", None),
        ),
        out_specs=P(None, "dom", "head"),
        check_vma=False,
    )
```

```python
import jax
import jax.numpy as jnp
from jax import lax
from jax.experimental import pallas as pl
from jax.experimental.pallas import tpu as pltpu
from jax.sharding import PartitionSpec as P

STEPS = 24
LP = 16
ROWS = STEPS * LP
HALF = ROWS // 2
TROWS = ROWS + 16
THALF = 208
LANES = 256
F32 = jnp.float32
BF16 = jnp.bfloat16
MESH = pl.DeviceIdType.MESH
NT = (((1,), (1,)), ((), ()))


def silu(v):
    return v / (1.0 + jnp.exp(-v))


def rel(j):
    return j + j // 2 - 2 * (j // 3)


def rcopy(src, dst, ssem, rsem, dev):
    return pltpu.make_async_remote_copy(
        src_ref=src,
        dst_ref=dst,
        send_sem=ssem,
        recv_sem=rsem,
        device_id=dev,
        device_id_type=MESH,
    )


def kernel(
    x_hbm,
    parents_hbm,
    vh_hbm,
    mh_hbm,
    gain_hbm,
    vk_hbm,
    vo_hbm,
    mk_hbm,
    mo_hbm,
    so_hbm,
    dlog_hbm,
    skip_hbm,
    ogain_hbm,
    step_hbm,
    v_hbm,
    mix_hbm,
    out_hbm,
    st_hbm,
    out_ref,
    parents,
    vh,
    mh,
    gain,
    vk,
    vo,
    mk,
    mo,
    so,
    dlog,
    skip,
    ogain,
    step_w,
    par,
    tok,
    vraw,
    vtmp,
    w,
    ms,
    wout,
    st,
    sbf,
    acc,
    accm,
    ss,
    hall,
    mixsend,
    mixrecv,
    bmat,
    call,
    ufar,
    ufarr,
    usend,
    urecv,
    sv4,
    m4,
    sqs,
    scaled,
    inv2s,
    sbuf,
    rbuf,
    hsend,
    hrecv,
    fsend,
    frecv,
    rsum,
    load_sem,
    small_sem,
    a_send,
    a_recv,
    as_send,
    as_recv,
    h_send,
    h_recv,
    m_send,
    m_recv,
    mf_send,
    c_send,
    c_recv,
    cs_send,
    cs_recv,
    u_send,
    u_recv,
    q_send,
    q_recv,
    r_send,
    r_recv,
    rs_send,
    rs_recv,
):
    d = lax.axis_index("dom")
    me = lax.axis_index("head")
    c = me % 2
    y = (me // 2) % 4
    z = me // 8
    s1 = 8 - 6 * c
    s2 = 2 + 6 * c
    p1 = z * (1 - c) + y * c
    p2 = y * (1 - c) + z * c
    sib = me + 1 - 2 * c

    def head(a, b):
        return {"head": a * s1 + b * s2 + c}

    def slot_own(i, k):
        return ((p1 + rel(i)) % 4) * s1 + ((p2 + rel(k)) % 4) * s2 + c

    def slot_sib(i, k):
        return ((p2 + rel(i)) % 4) * s2 + ((p1 + rel(k)) % 4) * s1 + 1 - c

    next1, prev1 = head((p1 + 1) % 4, p2), head((p1 + 3) % 4, p2)
    next2, prev2 = head(p1, (p2 + 1) % 4), head(p1, (p2 + 3) % 4)
    sibling = {"head": sib}

    def dom(o):
        return {"dom": (d + o) % 4}

    small = [
        pltpu.make_async_copy(src, dst, small_sem.at[n])
        for n, (src, dst) in enumerate(
            (
                (x_hbm, tok.at[me, pl.ds(0, ROWS)]),
                (gain_hbm, gain),
                (parents_hbm, parents),
                (vh_hbm, vh),
                (mh_hbm, mh),
                (vk_hbm, vk),
                (vo_hbm, vo),
                (mk_hbm, mk),
                (mo_hbm, mo),
                (so_hbm, so),
                (dlog_hbm, dlog),
                (skip_hbm, skip),
                (ogain_hbm, ogain),
                (step_hbm, step_w),
            )
        )
    ]
    for load in small:
        load.start()

    barrier = pltpu.get_barrier_semaphore()
    for dev in (next1, prev1, next2, prev2, sibling, dom(1), dom(2), dom(3)):
        pl.semaphore_signal(barrier, inc=1, device_id=dev, device_id_type=MESH)

    loads = []
    for i in range(8):
        rows = pl.ds(i * 4096, 4096)
        loads.append(
            pltpu.make_async_copy(v_hbm.at[rows], vraw.at[rows], load_sem.at[i])
        )
    loads.append(
        pltpu.make_async_copy(mix_hbm, ms.at[pl.ds(0, 64)], load_sem.at[8])
    )
    loads.append(pltpu.make_async_copy(st_hbm, st, load_sem.at[9]))
    loads.append(pltpu.make_async_copy(out_hbm, wout, load_sem.at[10]))
    for load in loads:
        load.start()
    for load in small:
        load.wait()
    tok[me, ROWS:TROWS] = jnp.broadcast_to(gain[...], (16, LANES)).astype(BF16)
    for n in range(3):
        rows = pl.ds(n * LP, LP)
        hall[d, rows, 0:256] = vh[rows, :].astype(BF16)
        hall[d, rows, 256:384] = jnp.concatenate(
            [mh[rows, :], jnp.zeros((LP, 64), F32)], 1
        ).astype(BF16)
    pl.semaphore_wait(barrier, 8)

    def ring(grp, idx, recv):
        k = (2, 2, 1, 1, 3, 3)[idx] if recv else (0, 0, 0, 0, 2, 1)[idx]
        slot = slot_own(k, 0) if grp == 4 else slot_own(grp, k)
        rows = (pl.ds(0, THALF), pl.ds(THALF, TROWS - THALF))[idx % 2]
        to = (next1, prev1) if grp == 4 else (next2, prev2)
        ref = tok.at[slot, rows]
        return rcopy(
            ref, ref, a_send.at[grp, idx], a_recv.at[grp, idx], to[(0, 0, 1, 1, 0, 1)[idx]]
        )

    def begin(grp, *idxs):
        for idx in idxs:
            ring(grp, idx, False).start()

    def got(grp, idx):
        ring(grp, idx, True).wait_recv()

    def to_sib(i, k, recv=False):
        slot = slot_sib(i, k) if recv else slot_own(i, k)
        ref = tok.at[slot]
        return rcopy(ref, ref, as_send.at[i * 4 + k], as_recv.at[i * 4 + k], sibling)

    begin(4, 0, 3)
    begin(0, 0, 3)
    begin(4, 1, 2)
    begin(0, 1, 2)
    to_sib(0, 0).start()

    hcopies = [
        rcopy(hall.at[d], hall.at[d], h_send.at[o - 1], h_recv.at[o - 1], dom(o))
        for o in (1, 2, 3)
    ]
    for copy in hcopies:
        copy.start()

    acc[...] = jnp.zeros_like(acc)
    accm[...] = jnp.zeros_like(accm)
    ss[...] = jnp.zeros_like(ss)
    ms[64:80, :] = jnp.concatenate(
        [step_w[...].astype(F32), jnp.zeros((12, 8192), F32)], 0
    ).astype(BF16)
    ms[80:128, :] = jnp.zeros((48, 8192), BF16)
    pi = lax.broadcasted_iota(jnp.int32, (64, 64), 0)
    pj = lax.broadcasted_iota(jnp.int32, (64, 64), 1)
    par[...] = jnp.broadcast_to(
        jnp.sum(jnp.where(pi == pj, parents[...].astype(F32), 0.0), 1, keepdims=True),
        (64, LANES),
    )

    def split(b, _):
        for u in range(2):
            v0 = pl.multiple_of((b * 2 + u) * 512, 512)
            vtmp[u] = vraw[pl.ds(v0, 512), :].astype(F32)
        for u in range(2):
            k0 = pl.multiple_of((b * 2 + u) * 128, 128)
            for j in range(2):
                for r in range(2):
                    lane = 256 * r + 128 * j
                    w[pl.ds(k0, 128), lane : lane + 128] = vtmp[
                        u, pl.ds(2 * j + r, 128, stride=4), :
                    ].astype(BF16)
        return 0

    for i in range(4):
        loads[i].wait()
    lax.fori_loop(0, 8, split, 0)
    got(4, 0)
    begin(4, 4)
    begin(2, 0, 2)
    got(4, 3)
    begin(4, 5)
    begin(1, 3, 1)
    lax.fori_loop(8, 16, split, 0)
    got(4, 1)
    begin(2, 3, 1)
    to_sib(2, 0).start()
    got(4, 2)
    begin(1, 0, 2)
    to_sib(1, 0).start()

    def pass_on(i):
        got(i, 0)
        begin(i, 4)
        got(i, 3)
        begin(i, 5)
        got(i, 1)
        to_sib(i, 2).start()
        got(i, 2)
        to_sib(i, 1).start()

    def far(i):
        got(i, 4)
        got(i, 5)
        to_sib(i, 3).start()

    for i in range(4, 8):
        loads[i].wait()
    lax.fori_loop(16, 24, split, 0)
    pass_on(0)
    lax.fori_loop(24, 32, split, 0)
    got(4, 4)
    begin(3, 0, 2)
    got(4, 5)
    begin(3, 3, 1)
    to_sib(3, 0).start()

    loads[8].wait()

    def project(i, k):
        to_sib(i, k, True).wait_recv()
        lhs, wide_rhs, narrow_rhs = [], [], []
        part = ss[...]
        for slot in (slot_own(i, k), slot_sib(i, k)):
            xf = tok[slot, 0:ROWS].astype(F32)
            grow = tok[slot, ROWS:TROWS].astype(F32)[0:1]
            sq = xf * xf
            part = part + sq[:, 0:128] + sq[:, 128:256]
            lhs.append((xf * grow).astype(BF16))
            k0 = pl.multiple_of(slot * 256, 256)
            wide_rhs.append(w[pl.ds(k0, 256), :])
            narrow_rhs.append(ms[:, pl.ds(k0, 256)])
        ss[...] = part
        xg = jnp.concatenate(lhs, 1)
        acc[...] += jnp.dot(
            xg, jnp.concatenate(wide_rhs, 0), preferred_element_type=F32
        )
        accm[...] += lax.dot_general(
            xg, jnp.concatenate(narrow_rhs, 1), NT, preferred_element_type=F32
        )

    def batch(count, which):
        def one(b, _):
            project(*which(b))
            return 0

        lax.fori_loop(0, count, one, 0)

    def cast(q, _):
        sbf[:, pl.ds(pl.multiple_of(q * 256, 256), 256)] = st[q].astype(BF16)
        return 0

    batch(1, lambda b: (b, 0))
    pass_on(1)
    batch(1, lambda b: (b + 1, 0))
    pass_on(2)
    loads[9].wait()
    lax.fori_loop(0, LP, cast, 0)
    far(0)
    batch(2, lambda b: (2 + b, 0))
    pass_on(3)
    batch(3, lambda b: (0, b + 1))
    far(1)
    batch(2, lambda b: (1, b + 1))
    far(2)
    batch(3, lambda b: (1 + (b + 2) // 3, 3 * (1 - (b + 2) // 3) + b))
    batch(3, lambda b: (2 + (b + 1) // 2, 3 * (1 - (b + 1) // 2) + b))
    far(3)
    batch(1, lambda b: (3 + b, 3))

    inv = lax.rsqrt(jnp.sum(ss[...], axis=1, keepdims=True) / 8192.0 + 1e-5)

    for copy in hcopies:
        copy.wait()
    hi = lax.broadcasted_iota(jnp.int32, (LP, 192), 1)
    same = par[pl.ds(pl.multiple_of(d * LP, LP), LP), 0:192] == (
        (hi // 48) * LP + hi % LP
    ).astype(F32)
    hot = jnp.concatenate(
        [
            jnp.where(same & ((hi // LP) % 3 == n), 1.0, 0.0).astype(BF16)
            for n in range(3)
        ],
        0,
    )
    hprev = jnp.dot(hot, hall[...].reshape(192, 384), preferred_element_type=F32)
    mtile = accm[...] * inv

    def conv(window, taps, bias):
        total = bias
        for k in range(4):
            total = total + taps[k : k + 1] * window[k * LP : k * LP + ROWS]
        return silu(total)

    wide4 = jnp.zeros((4, 64), F32)
    mact = conv(
        jnp.concatenate([hprev[:, 256:384], mtile], 0),
        jnp.concatenate([mk[...], wide4], 1),
        jnp.concatenate([mo[...], wide4[0:1]], 1),
    )
    low = lax.broadcasted_iota(jnp.int32, (HALF, 128), 1) < 64
    mixsend[...] = jnp.where(
        low, mact[0:HALF], pltpu.roll(mact[HALF:ROWS], 64, 1)
    ).astype(BF16)
    first = ((me % 16) // 4) * 8 + c
    place = (me // 16) * 4 + me % 4

    def mix_copy(n):
        return rcopy(
            mixsend, mixrecv.at[place], m_send.at[n], m_recv.at[place], {"head": first + 2 * n}
        )

    @pl.loop(0, 4)
    def _(n):
        @pl.when(first + 2 * n != me)
        def _():
            mix_copy(n).start()

        @pl.when(first + 2 * n == me)
        def _():
            pltpu.make_async_copy(mixsend, mixrecv.at[place], m_recv.at[place]).start()

    def mix_pass(n):
        return rcopy(mixrecv.at[n], mixrecv.at[n], mf_send.at[n], m_recv.at[n], sibling)

    value = acc[:, 256:512] * inv
    vact = conv(jnp.concatenate([hprev[:, 0:256], value], 0), vk, vo[...])
    row = lax.broadcasted_iota(jnp.int32, (1, 128), 1)

    def heads_row(ref):
        out = jnp.zeros((1, 128), F32)
        for h in range(4):
            out = jnp.where(row == 64 + h, ref[0:1, h : h + 1], out)
        return out

    step = mtile + heads_row(so)
    step = jnp.maximum(step, 0.0) + jnp.log1p(jnp.exp(-jnp.abs(step)))
    run = -step * jnp.exp(heads_row(dlog))
    for sh in (1, 2, 4, 8, 16):
        z0 = jnp.zeros((sh * LP, 128), F32)
        run = run + jnp.concatenate([z0, run[: ROWS - sh * LP]], 0)
    run_t = run.T
    lane = lax.broadcasted_iota(jnp.int32, (ROWS, LANES), 1)

    def spread(t, at=64):
        out = jnp.broadcast_to(t[:, at + 3 : at + 4], (t.shape[0], LANES))
        for h in (2, 1, 0):
            out = jnp.where(
                lane[0 : t.shape[0]] < 64 * h + 64, t[:, at + h : at + h + 1], out
            )
        return out

    for n in (4, 6):
        mix_pass(n + c).wait_recv()
        mix_pass(n + c).start()
    for n in (4, 6):
        mix_pass(n + 1 - c).wait_recv()

    def assemble(first_slot, dst):
        for t in range(2):
            a = mixrecv[first_slot + 2 * t].astype(F32)
            b = mixrecv[first_slot + 2 * t + 1].astype(F32)
            dst[0:HALF, 128 * t : 128 * t + 128] = jnp.where(
                low, a, pltpu.roll(b, 64, 1)
            ).astype(BF16)
            dst[HALF:ROWS, 128 * t : 128 * t + 128] = jnp.where(
                low, pltpu.roll(a, 64, 1), b
            ).astype(BF16)

    cmat = call.at[d]
    assemble(4, cmat)
    x0 = pl.multiple_of(c * HALF, HALF)
    quarter = HALF // 2

    def c_copy(idx, recv):
        e = (d + ((3, 1, 2, 2)[idx] if recv else (0, 0, 3, 1)[idx])) % 4
        rows = (
            pl.ds(x0, HALF),
            pl.ds(x0, HALF),
            pl.ds(x0, quarter),
            pl.ds(x0 + quarter, quarter),
        )[idx]
        ref = call.at[e, rows]
        return rcopy(ref, ref, c_send.at[idx], c_recv.at[idx], dom((1, 3)[idx % 2]))

    def c_pass(o, recv):
        start = pl.multiple_of((1 - c) * HALF, HALF) if recv else x0
        ref = call.at[(d + o) % 4, pl.ds(start, HALF)]
        return rcopy(ref, ref, cs_send.at[o - 1], cs_recv.at[o - 1], sibling)

    c_copy(0, False).start()
    c_copy(1, False).start()
    for n in (0, 2):
        mix_pass(n + c).wait_recv()
        mix_pass(n + c).start()

    def reads(e):
        mine = par[pl.ds(pl.multiple_of(e * LP, LP), LP), :]

        cval = call[e].reshape(STEPS, LP, LANES)
        lhs = []
        for n in range(LP):
            q = (d * LP + n).astype(F32)
            mask = jnp.where(mine == q, 1.0, 0.0).astype(BF16)
            lhs.append((cval * mask[None]).reshape(ROWS, LANES))
        return lax.dot_general(
            jnp.concatenate(lhs, 1), sbf[...], NT, preferred_element_type=F32
        )

    start_read = reads(d)
    for idx, o in ((0, 3), (1, 1)):
        c_copy(idx, True).wait_recv()
        c_copy(2 + idx, False).start()
        c_pass(o, False).start()
    for n in (0, 2):
        mix_pass(n + 1 - c).wait_recv()
    assemble(0, bmat)
    gram = lax.dot_general(cmat[...], bmat[...], NT, preferred_element_type=F32)
    gact = silu(acc[:, 0:256] * inv)
    c_copy(2, True).wait_recv()
    c_copy(3, True).wait_recv()
    c_pass(2, False).start()
    c_pass(2, True).wait_recv()
    ufar[...] = reads((d + 2) % 4).astype(BF16)

    def u_half(top):
        rows = pl.ds(0 if top else HALF, HALF)
        n = 0 if top else 1
        return rcopy(
            ufar.at[rows], ufarr.at[rows], u_send.at[n], u_recv.at[n], dom(1 if top else 3)
        )

    def u_full(n, top):
        rows = pl.ds(0 if top else HALF, HALF)
        m = 2 + 2 * n + (0 if top else 1)
        return rcopy(
            usend.at[n, rows], urecv.at[n, rows], u_send.at[m], u_recv.at[m], dom(1 + 2 * n)
        )

    u_half(True).start()
    u_half(False).start()
    c_pass(1, True).wait_recv()
    usend[0] = reads((d + 1) % 4).astype(BF16)
    u_full(0, False).start()
    c_pass(3, True).wait_recv()
    usend[1] = reads((d + 3) % 4).astype(BF16)
    u_full(1, True).start()
    u_half(True).wait_recv()
    usend[0, 0:HALF] = usend[0, 0:HALF] + ufarr[0:HALF]
    u_full(0, True).start()
    u_half(False).wait_recv()
    usend[1, HALF:ROWS] = usend[1, HALF:ROWS] + ufarr[HALF:ROWS]
    u_full(1, False).start()

    sv = vact * spread(step)
    for h in range(4):
        inside = (lane >= 64 * h) & (lane < 64 * h + 64)
        sv4[h * ROWS : (h + 1) * ROWS, :] = jnp.where(inside, sv, 0.0).astype(BF16)
    gi = lax.broadcasted_iota(jnp.int32, (ROWS, ROWS), 0)
    gj = lax.broadcasted_iota(jnp.int32, (ROWS, ROWS), 1)
    keep = ((gi % LP) == (gj % LP)) & (gj <= gi)
    for h in range(4):
        diff = jnp.where(keep, run[:, 64 + h : 65 + h] - run_t[64 + h : 65 + h, :], -1e30)
        m4[:, h * ROWS : (h + 1) * ROWS] = (gram * jnp.exp(diff)).astype(BF16)
    inner = jnp.dot(m4[...], sv4[...], preferred_element_type=F32)
    inner = inner + spread(skip[...], 0) * vact
    carry = spread(jnp.exp(run))
    for n in range(2):
        for top in (True, False):
            u_full(n, top).wait_recv()
    start_read = start_read + urecv[0].astype(F32) + urecv[1].astype(F32)
    total = (inner + carry * start_read) * gact
    scaled[...] = (total * ogain[...]).astype(BF16)
    sq = lax.dot_general(
        jnp.ones((8, LANES), F32),
        total * total,
        NT,
        preferred_element_type=F32,
        precision=lax.Precision.HIGHEST,
    )
    place8 = me % 8
    sqs[place8] = sq

    def sq_copy(o):
        at = (place8 + o) % 8
        return rcopy(
            sqs.at[place8], sqs.at[place8], q_send.at[o - 1], q_recv.at[o - 1], {"head": z * 8 + at}
        )

    for o in range(1, 8):
        sq_copy(o).start()

    loads[10].wait()

    def terms(slot):
        return jnp.dot(
            scaled[...],
            wout[:, pl.ds(pl.multiple_of(slot * 256, 256), 256)],
            preferred_element_type=F32,
        )

    def sib_terms(n):
        return rcopy(sbuf.at[n], rbuf.at[n], rs_send.at[n], rs_recv.at[n], sibling)

    def give(*blocks):
        made = [terms(slot_sib(i, k)).astype(BF16) for i, k in blocks]
        for (i, k), block in zip(blocks, made):
            sbuf[i * 4 + k] = block
        for i, k in blocks:
            sib_terms(i * 4 + k).start()

    give((3, 3), (2, 3))
    give((1, 3), (0, 3))

    @pl.loop(0, 4)
    def _(t):
        give((3 - t, 1), (3 - t, 2))

    for o in range(1, 8):
        at = (place8 + 8 - o) % 8
        rcopy(sqs.at[at], sqs.at[at], q_send.at[o - 1], q_recv.at[o - 1], sibling).wait_recv()
    tsq = sqs[0]
    for o in range(1, 8):
        tsq = tsq + sqs[o]
    inv2 = lax.rsqrt(tsq.T[:, 0:1] / 2048.0 + 1e-5)
    inv2s[...] = jnp.broadcast_to(inv2, (ROWS, LANES))

    def finish(own, i, k):
        sib_terms(i * 4 + k).wait_recv()
        return (own + rbuf[i * 4 + k].astype(F32)) * inv2s[...]

    def half_copy(i, top, to):
        rows = pl.ds(0 if top else HALF, HALF)
        n = 0 if top else 1
        return rcopy(hsend.at[i, rows], hrecv.at[i, rows], r_send.at[i, n], r_recv.at[i, n], to)

    def full_copy(i, n, to):
        return rcopy(
            fsend.at[2 * i + n], frecv.at[2 * i + n], r_send.at[i, 2 + n], r_recv.at[i, 2 + n], to
        )

    @pl.loop(0, 4)
    def _(t):
        i = 3 - t
        hsend[i] = finish(terms(slot_own(i, 3)), i, 3).astype(BF16)
        half_copy(i, True, next2).start()
        half_copy(i, False, prev2).start()

    @pl.loop(0, 4)
    def _(t):
        i = 3 - t
        a = terms(slot_own(i, 1))
        b = terms(slot_own(i, 2))
        give((i, 0),)
        a = finish(a, i, 1)
        half_copy(i, True, next2).wait_recv()
        fsend[2 * i, 0:HALF] = (a[0:HALF] + hrecv[i, 0:HALF].astype(F32)).astype(BF16)
        fsend[2 * i, HALF:ROWS] = a[HALF:ROWS].astype(BF16)
        full_copy(i, 0, next2).start()
        b = finish(b, i, 2)
        half_copy(i, False, prev2).wait_recv()
        fsend[2 * i + 1, 0:HALF] = b[0:HALF].astype(BF16)
        fsend[2 * i + 1, HALF:ROWS] = (
            b[HALF:ROWS] + hrecv[i, HALF:ROWS].astype(F32)
        ).astype(BF16)
        full_copy(i, 1, prev2).start()

    @pl.loop(0, 4)
    def _(t):
        i = 3 - t
        rsum[i] = finish(terms(slot_own(i, 0)), i, 0)

    def column(i):
        full_copy(i, 0, next2).wait_recv()
        full_copy(i, 1, prev2).wait_recv()
        return rsum[i] + frecv[2 * i].astype(F32) + frecv[2 * i + 1].astype(F32)

    hsend[4] = column(3).astype(BF16)
    half_copy(4, True, next1).start()
    half_copy(4, False, prev1).start()

    def last_copy(n, top):
        rows = pl.ds(0 if top else HALF, HALF)
        m = 2 + 2 * n + (0 if top else 1)
        return rcopy(
            fsend.at[8 + n, rows],
            frecv.at[8 + n, rows],
            r_send.at[4, m],
            r_recv.at[4, m],
            (next1, prev1)[n],
        )

    b = column(2)
    fsend[9, 0:HALF] = b[0:HALF].astype(BF16)
    last_copy(1, True).start()
    a = column(1)
    fsend[8, HALF:ROWS] = a[HALF:ROWS].astype(BF16)
    last_copy(0, False).start()
    half_copy(4, True, next1).wait_recv()
    fsend[8, 0:HALF] = (a[0:HALF] + hrecv[4, 0:HALF].astype(F32)).astype(BF16)
    last_copy(0, True).start()
    half_copy(4, False, prev1).wait_recv()
    fsend[9, HALF:ROWS] = (b[HALF:ROWS] + hrecv[4, HALF:ROWS].astype(F32)).astype(BF16)
    last_copy(1, False).start()
    a = column(0)
    for n in range(2):
        for top in (True, False):
            last_copy(n, top).wait_recv()
    out_ref[...] = (a + frecv[8].astype(F32) + frecv[9].astype(F32)).astype(BF16)

    for grp in range(5):
        for idx in range(6):
            ring(grp, idx, False).wait_send()

    @pl.loop(0, 16)
    def _(n):
        to_sib(n // 4, n % 4).wait_send()
        sib_terms(n).wait_send()

    @pl.loop(0, 4)
    def _(n):
        @pl.when(first + 2 * n != me)
        def _():
            mix_copy(n).wait_send()

        mix_pass(2 * n + c).wait_send()

    for idx in range(4):
        c_copy(idx, False).wait_send()
    for o in (1, 2, 3):
        c_pass(o, False).wait_send()
    for flag in (0, 1):
        u_half(flag == 0).wait_send()
        u_full(flag, True).wait_send()
        u_full(flag, False).wait_send()
    for o in range(1, 8):
        sq_copy(o).wait_send()
    for i in range(5):
        nxt, prv = (next1, prev1) if i == 4 else (next2, prev2)
        half_copy(i, True, nxt).wait_send()
        half_copy(i, False, prv).wait_send()
        if i == 4:
            for n in range(2):
                last_copy(n, True).wait_send()
                last_copy(n, False).wait_send()
        else:
            full_copy(i, 0, nxt).wait_send()
            full_copy(i, 1, prv).wait_send()


def body(
    tokens,
    parents,
    state,
    vhist,
    mhist,
    gain,
    gvw,
    mw,
    sw,
    vk,
    vo,
    mk,
    mo,
    so,
    dlog,
    skip,
    ogain,
    ow,
):
    v = gvw.reshape(8192, 2, 2, 128).transpose(0, 2, 1, 3).reshape(32768, 128)

    vmem = pl.BlockSpec(memory_space=pltpu.VMEM)
    hbm = pl.BlockSpec(memory_space=pl.ANY)
    dma = pltpu.SemaphoreType.DMA
    big = (ROWS, LANES)
    out = pl.pallas_call(
        kernel,
        out_shape=jax.ShapeDtypeStruct(big, BF16),
        in_specs=[hbm] * 18,
        out_specs=vmem,
        scratch_shapes=[
            pltpu.VMEM((1, 64), jnp.int32),
            pltpu.VMEM((48, 256), F32),
            pltpu.VMEM((48, 64), F32),
            pltpu.VMEM((1, 256), F32),
            pltpu.VMEM((4, 256), F32),
            pltpu.VMEM((1, 256), F32),
            pltpu.VMEM((4, 64), F32),
            pltpu.VMEM((1, 64), F32),
            pltpu.VMEM((1, 4), F32),
            pltpu.VMEM((1, 4), F32),
            pltpu.VMEM((1, 4), F32),
            pltpu.VMEM((1, 256), F32),
            pltpu.VMEM((4, 8192), BF16),
            pltpu.VMEM((64, LANES), F32),
            pltpu.VMEM((32, TROWS, LANES), BF16),
            pltpu.VMEM((32768, 128), BF16),
            pltpu.VMEM((2, 512, 128), F32),
            pltpu.VMEM((8192, 512), BF16),
            pltpu.VMEM((128, 8192), BF16),
            pltpu.VMEM((256, 8192), BF16),
            pltpu.VMEM((LP, 256, 256), F32),
            pltpu.VMEM((256, LP * 256), BF16),
            pltpu.VMEM((ROWS, 512), F32),
            pltpu.VMEM((ROWS, 128), F32),
            pltpu.VMEM((ROWS, 128), F32),
            pltpu.VMEM((4, 48, 384), BF16),
            pltpu.VMEM((HALF, 128), BF16),
            pltpu.VMEM((8, HALF, 128), BF16),
            pltpu.VMEM(big, BF16),
            pltpu.VMEM((4, *big), BF16),
            pltpu.VMEM(big, BF16),
            pltpu.VMEM(big, BF16),
            pltpu.VMEM((2, *big), BF16),
            pltpu.VMEM((2, *big), BF16),
            pltpu.VMEM((4 * ROWS, LANES), BF16),
            pltpu.VMEM((ROWS, 4 * ROWS), BF16),
            pltpu.VMEM((8, 8, ROWS), F32),
            pltpu.VMEM(big, BF16),
            pltpu.VMEM(big, F32),
            pltpu.VMEM((16, *big), BF16),
            pltpu.VMEM((16, *big), BF16),
            pltpu.VMEM((5, *big), BF16),
            pltpu.VMEM((5, *big), BF16),
            pltpu.VMEM((10, *big), BF16),
            pltpu.VMEM((10, *big), BF16),
            pltpu.VMEM((4, *big), F32),
            dma((11,)),
            dma((14,)),
            dma((5, 6)),
            dma((5, 6)),
            dma((16,)),
            dma((16,)),
            dma((3,)),
            dma((3,)),
            dma((4,)),
            dma((8,)),
            dma((8,)),
            dma((4,)),
            dma((4,)),
            dma((3,)),
            dma((3,)),
            dma((6,)),
            dma((6,)),
            dma((7,)),
            dma((7,)),
            dma((5, 6)),
            dma((5, 6)),
            dma((16,)),
            dma((16,)),
        ],
        compiler_params=pltpu.CompilerParams(
            collective_id=0,
            has_side_effects=True,
            vmem_limit_bytes=63 * 1024 * 1024,
        ),
    )(
        tokens.reshape(ROWS, LANES),
        parents.reshape(1, 64),
        vhist.transpose(1, 0, 2).reshape(48, LANES),
        mhist.transpose(1, 0, 2).reshape(48, 64),
        gain.reshape(1, LANES),
        vk,
        vo.reshape(1, LANES),
        mk,
        mo.reshape(1, 64),
        so.reshape(1, 4),
        dlog.reshape(1, 4),
        skip.reshape(1, 4),
        ogain.reshape(1, LANES),
        sw.T,
        v,
        mw.T,
        ow,
        state.reshape(LP, 256, 256),
    )
    return out.reshape(STEPS, LP, LANES)


def solution(mesh):
    return jax.shard_map(
        body,
        mesh=mesh,
        in_specs=(
            P(None, "dom", "head"),
            P(),
            P("dom", "head", None, None),
            P("dom", None, "head"),
            P("dom", None, "head"),
            P("head"),
            P(None, None, "head"),
            P(None, "head"),
            P(None, "head"),
            P(None, "head"),
            P("head"),
            P(None, "head"),
            P("head"),
            P("head"),
            P("head"),
            P("head"),
            P("head"),
            P("head", None),
        ),
        out_specs=P(None, "dom", "head"),
        check_vma=False,
    )
```

```python
import jax
import jax.numpy as jnp
from jax import lax
from jax.experimental import pallas as pl
from jax.experimental.pallas import tpu as pltpu
from jax.sharding import PartitionSpec as P

STEPS = 24
LP = 16
ROWS = STEPS * LP
HALF = ROWS // 2
TROWS = ROWS + 16
THALF = 208
LANES = 256
F32 = jnp.float32
BF16 = jnp.bfloat16
MESH = pl.DeviceIdType.MESH
NT = (((1,), (1,)), ((), ()))


def silu(v):
    return v / (1.0 + jnp.exp(-v))


def rel(j):
    return j + j // 2 - 2 * (j // 3)


def rcopy(src, dst, ssem, rsem, dev):
    return pltpu.make_async_remote_copy(
        src_ref=src,
        dst_ref=dst,
        send_sem=ssem,
        recv_sem=rsem,
        device_id=dev,
        device_id_type=MESH,
    )


def kernel(
    x_hbm,
    parents_hbm,
    vh_hbm,
    mh_hbm,
    gain_hbm,
    vk_hbm,
    vo_hbm,
    mk_hbm,
    mo_hbm,
    so_hbm,
    dlog_hbm,
    skip_hbm,
    ogain_hbm,
    step_hbm,
    v_hbm,
    mix_hbm,
    out_hbm,
    st_hbm,
    out_ref,
    parents,
    vh,
    mh,
    gain,
    vk,
    vo,
    mk,
    mo,
    so,
    dlog,
    skip,
    ogain,
    step_w,
    par,
    tok,
    vraw,
    vtmp,
    w,
    ms,
    wout,
    st,
    sbf,
    acc,
    accm,
    ss,
    hall,
    mixsend,
    mixrecv,
    bmat,
    call,
    ufar,
    ufarr,
    usend,
    urecv,
    sv4,
    m4,
    sqs,
    scaled,
    inv2s,
    sbuf,
    rbuf,
    hsend,
    hrecv,
    fsend,
    frecv,
    rsum,
    load_sem,
    small_sem,
    a_send,
    a_recv,
    as_send,
    as_recv,
    h_send,
    h_recv,
    m_send,
    m_recv,
    mf_send,
    c_send,
    c_recv,
    cs_send,
    cs_recv,
    u_send,
    u_recv,
    q_send,
    q_recv,
    r_send,
    r_recv,
    rs_send,
    rs_recv,
):
    d = lax.axis_index("dom")
    me = lax.axis_index("head")
    c = me % 2
    y = (me // 2) % 4
    z = me // 8
    s1 = 8 - 6 * c
    s2 = 2 + 6 * c
    p1 = z * (1 - c) + y * c
    p2 = y * (1 - c) + z * c
    sib = me + 1 - 2 * c

    def head(a, b):
        return {"head": a * s1 + b * s2 + c}

    def slot_own(i, k):
        return ((p1 + rel(i)) % 4) * s1 + ((p2 + rel(k)) % 4) * s2 + c

    def slot_sib(i, k):
        return ((p2 + rel(i)) % 4) * s2 + ((p1 + rel(k)) % 4) * s1 + 1 - c

    next1, prev1 = head((p1 + 1) % 4, p2), head((p1 + 3) % 4, p2)
    next2, prev2 = head(p1, (p2 + 1) % 4), head(p1, (p2 + 3) % 4)
    sibling = {"head": sib}

    def dom(o):
        return {"dom": (d + o) % 4}

    small = [
        pltpu.make_async_copy(src, dst, small_sem.at[n])
        for n, (src, dst) in enumerate(
            (
                (x_hbm, tok.at[me, pl.ds(0, ROWS)]),
                (gain_hbm, gain),
                (parents_hbm, parents),
                (vh_hbm, vh),
                (mh_hbm, mh),
                (vk_hbm, vk),
                (vo_hbm, vo),
                (mk_hbm, mk),
                (mo_hbm, mo),
                (so_hbm, so),
                (dlog_hbm, dlog),
                (skip_hbm, skip),
                (ogain_hbm, ogain),
                (step_hbm, step_w),
            )
        )
    ]
    for load in small:
        load.start()

    barrier = pltpu.get_barrier_semaphore()
    for dev in (next1, prev1, next2, prev2, sibling, dom(1), dom(2), dom(3)):
        pl.semaphore_signal(barrier, inc=1, device_id=dev, device_id_type=MESH)

    loads = []
    for i in range(8):
        rows = pl.ds(i * 4096, 4096)
        loads.append(
            pltpu.make_async_copy(v_hbm.at[rows], vraw.at[rows], load_sem.at[i])
        )
    loads.append(
        pltpu.make_async_copy(mix_hbm, ms.at[pl.ds(0, 64)], load_sem.at[8])
    )
    loads.append(pltpu.make_async_copy(st_hbm, st, load_sem.at[9]))
    loads.append(pltpu.make_async_copy(out_hbm, wout, load_sem.at[10]))
    for load in loads:
        load.start()
    for load in small:
        load.wait()
    tok[me, ROWS:TROWS] = jnp.broadcast_to(gain[...], (16, LANES)).astype(BF16)
    for n in range(3):
        rows = pl.ds(n * LP, LP)
        hall[d, rows, 0:256] = vh[rows, :].astype(BF16)
        hall[d, rows, 256:384] = jnp.concatenate(
            [mh[rows, :], jnp.zeros((LP, 64), F32)], 1
        ).astype(BF16)
    pl.semaphore_wait(barrier, 8)

    def ring(grp, idx, recv):
        k = (2, 2, 1, 1, 3, 3)[idx] if recv else (0, 0, 0, 0, 2, 1)[idx]
        slot = slot_own(k, 0) if grp == 4 else slot_own(grp, k)
        rows = (pl.ds(0, THALF), pl.ds(THALF, TROWS - THALF))[idx % 2]
        to = (next1, prev1) if grp == 4 else (next2, prev2)
        ref = tok.at[slot, rows]
        return rcopy(
            ref, ref, a_send.at[grp, idx], a_recv.at[grp, idx], to[(0, 0, 1, 1, 0, 1)[idx]]
        )

    def begin(grp, *idxs):
        for idx in idxs:
            ring(grp, idx, False).start()

    def got(grp, idx):
        ring(grp, idx, True).wait_recv()

    def to_sib(i, k, recv=False):
        slot = slot_sib(i, k) if recv else slot_own(i, k)
        ref = tok.at[slot]
        return rcopy(ref, ref, as_send.at[i * 4 + k], as_recv.at[i * 4 + k], sibling)

    begin(4, 0, 3)
    begin(4, 1, 2)
    to_sib(0, 0).start()

    hcopies = [
        rcopy(hall.at[d], hall.at[d], h_send.at[o - 1], h_recv.at[o - 1], dom(o))
        for o in (1, 2, 3)
    ]
    for copy in hcopies:
        copy.start()

    acc[...] = jnp.zeros_like(acc)
    accm[...] = jnp.zeros_like(accm)
    ss[...] = jnp.zeros_like(ss)
    ms[64:80, :] = jnp.concatenate(
        [step_w[...].astype(F32), jnp.zeros((12, 8192), F32)], 0
    ).astype(BF16)
    ms[80:128, :] = jnp.zeros((48, 8192), BF16)
    pi = lax.broadcasted_iota(jnp.int32, (64, 64), 0)
    pj = lax.broadcasted_iota(jnp.int32, (64, 64), 1)
    par[...] = jnp.broadcast_to(
        jnp.sum(jnp.where(pi == pj, parents[...].astype(F32), 0.0), 1, keepdims=True),
        (64, LANES),
    )

    def split(b, _):
        for u in range(2):
            v0 = pl.multiple_of((b * 2 + u) * 512, 512)
            vtmp[u] = vraw[pl.ds(v0, 512), :].astype(F32)
        for u in range(2):
            k0 = pl.multiple_of((b * 2 + u) * 128, 128)
            for j in range(2):
                for r in range(2):
                    lane = 256 * r + 128 * j
                    w[pl.ds(k0, 128), lane : lane + 128] = vtmp[
                        u, pl.ds(2 * j + r, 128, stride=4), :
                    ].astype(BF16)
        return 0

    for i in range(4):
        loads[i].wait()
    begin(0, 0, 3)
    begin(0, 1, 2)
    lax.fori_loop(0, 8, split, 0)
    got(4, 0)
    begin(4, 4)
    begin(2, 0, 2)
    got(4, 3)
    begin(4, 5)
    begin(1, 3, 1)
    lax.fori_loop(8, 16, split, 0)
    got(4, 1)
    begin(2, 3, 1)
    to_sib(2, 0).start()
    got(4, 2)
    begin(1, 0, 2)
    to_sib(1, 0).start()

    def pass_on(i):
        got(i, 0)
        begin(i, 4)
        got(i, 3)
        begin(i, 5)
        got(i, 1)
        to_sib(i, 2).start()
        got(i, 2)
        to_sib(i, 1).start()

    def far(i):
        got(i, 4)
        got(i, 5)
        to_sib(i, 3).start()

    for i in range(4, 8):
        loads[i].wait()
    lax.fori_loop(16, 24, split, 0)
    pass_on(0)
    lax.fori_loop(24, 32, split, 0)
    got(4, 4)
    begin(3, 0, 2)
    got(4, 5)
    begin(3, 3, 1)
    to_sib(3, 0).start()

    loads[8].wait()

    def project(i, k):
        to_sib(i, k, True).wait_recv()
        lhs, wide_rhs, narrow_rhs = [], [], []
        part = ss[...]
        for slot in (slot_own(i, k), slot_sib(i, k)):
            xf = tok[slot, 0:ROWS].astype(F32)
            grow = tok[slot, ROWS:TROWS].astype(F32)[0:1]
            sq = xf * xf
            part = part + sq[:, 0:128] + sq[:, 128:256]
            lhs.append((xf * grow).astype(BF16))
            k0 = pl.multiple_of(slot * 256, 256)
            wide_rhs.append(w[pl.ds(k0, 256), :])
            narrow_rhs.append(ms[:, pl.ds(k0, 256)])
        ss[...] = part
        xg = jnp.concatenate(lhs, 1)
        acc[...] += jnp.dot(
            xg, jnp.concatenate(wide_rhs, 0), preferred_element_type=F32
        )
        accm[...] += lax.dot_general(
            xg, jnp.concatenate(narrow_rhs, 1), NT, preferred_element_type=F32
        )

    def batch(count, which):
        def one(b, _):
            project(*which(b))
            return 0

        lax.fori_loop(0, count, one, 0)

    def cast(q, _):
        sbf[:, pl.ds(pl.multiple_of(q * 256, 256), 256)] = st[q].astype(BF16)
        return 0

    def pairs(*blocks):
        (i0, k0), n = blocks[0], len(blocks)
        di, dk = (blocks[1][0] - i0, blocks[1][1] - k0) if n > 1 else (0, 0)
        batch(n, lambda b: (i0 + di * b, k0 + dk * b))

    pairs((0, 0), (1, 0))
    got(1, 0)
    begin(1, 4)
    got(1, 3)
    begin(1, 5)
    pairs((0, 1), (0, 2))
    got(2, 0)
    begin(2, 4)
    got(2, 3)
    begin(2, 5)
    got(1, 1)
    to_sib(1, 2).start()
    got(1, 2)
    to_sib(1, 1).start()
    pairs((2, 0), (3, 0))
    got(2, 1)
    to_sib(2, 2).start()
    got(2, 2)
    to_sib(2, 1).start()
    far(0)
    loads[9].wait()
    lax.fori_loop(0, LP, cast, 0)
    pairs((1, 1), (1, 2))
    got(3, 0)
    begin(3, 4)
    got(3, 3)
    begin(3, 5)
    pairs((2, 1), (2, 2))
    got(3, 1)
    to_sib(3, 2).start()
    got(3, 2)
    to_sib(3, 1).start()
    far(1)
    pairs((0, 3),)
    far(2)
    pairs((1, 3),)
    pairs((3, 1), (3, 2))
    far(3)
    pairs((2, 3), (3, 3))

    inv = lax.rsqrt(jnp.sum(ss[...], axis=1, keepdims=True) / 8192.0 + 1e-5)

    for copy in hcopies:
        copy.wait()
    hi = lax.broadcasted_iota(jnp.int32, (LP, 192), 1)
    same = par[pl.ds(pl.multiple_of(d * LP, LP), LP), 0:192] == (
        (hi // 48) * LP + hi % LP
    ).astype(F32)
    hot = jnp.concatenate(
        [
            jnp.where(same & ((hi // LP) % 3 == n), 1.0, 0.0).astype(BF16)
            for n in range(3)
        ],
        0,
    )
    hprev = jnp.dot(hot, hall[...].reshape(192, 384), preferred_element_type=F32)
    mtile = accm[...] * inv

    def conv(window, taps, bias):
        total = bias
        for k in range(4):
            total = total + taps[k : k + 1] * window[k * LP : k * LP + ROWS]
        return silu(total)

    wide4 = jnp.zeros((4, 64), F32)
    mact = conv(
        jnp.concatenate([hprev[:, 256:384], mtile], 0),
        jnp.concatenate([mk[...], wide4], 1),
        jnp.concatenate([mo[...], wide4[0:1]], 1),
    )
    low = lax.broadcasted_iota(jnp.int32, (HALF, 128), 1) < 64
    mixsend[...] = jnp.where(
        low, mact[0:HALF], pltpu.roll(mact[HALF:ROWS], 64, 1)
    ).astype(BF16)
    first = ((me % 16) // 4) * 8 + c
    place = (me // 16) * 4 + me % 4

    def mix_copy(n):
        return rcopy(
            mixsend, mixrecv.at[place], m_send.at[n], m_recv.at[place], {"head": first + 2 * n}
        )

    @pl.loop(0, 4)
    def _(n):
        @pl.when(first + 2 * n != me)
        def _():
            mix_copy(n).start()

        @pl.when(first + 2 * n == me)
        def _():
            pltpu.make_async_copy(mixsend, mixrecv.at[place], m_recv.at[place]).start()

    def mix_pass(n):
        return rcopy(mixrecv.at[n], mixrecv.at[n], mf_send.at[n], m_recv.at[n], sibling)

    value = acc[:, 256:512] * inv
    vact = conv(jnp.concatenate([hprev[:, 0:256], value], 0), vk, vo[...])
    row = lax.broadcasted_iota(jnp.int32, (1, 128), 1)

    def heads_row(ref):
        out = jnp.zeros((1, 128), F32)
        for h in range(4):
            out = jnp.where(row == 64 + h, ref[0:1, h : h + 1], out)
        return out

    step = mtile + heads_row(so)
    step = jnp.maximum(step, 0.0) + jnp.log1p(jnp.exp(-jnp.abs(step)))
    run = -step * jnp.exp(heads_row(dlog))
    for sh in (1, 2, 4, 8, 16):
        z0 = jnp.zeros((sh * LP, 128), F32)
        run = run + jnp.concatenate([z0, run[: ROWS - sh * LP]], 0)
    run_t = run.T
    lane = lax.broadcasted_iota(jnp.int32, (ROWS, LANES), 1)

    def spread(t, at=64):
        out = jnp.broadcast_to(t[:, at + 3 : at + 4], (t.shape[0], LANES))
        for h in (2, 1, 0):
            out = jnp.where(
                lane[0 : t.shape[0]] < 64 * h + 64, t[:, at + h : at + h + 1], out
            )
        return out

    for n in (4, 6):
        mix_pass(n + c).wait_recv()
        mix_pass(n + c).start()
    for n in (4, 6):
        mix_pass(n + 1 - c).wait_recv()

    def assemble(first_slot, dst):
        for t in range(2):
            a = mixrecv[first_slot + 2 * t].astype(F32)
            b = mixrecv[first_slot + 2 * t + 1].astype(F32)
            dst[0:HALF, 128 * t : 128 * t + 128] = jnp.where(
                low, a, pltpu.roll(b, 64, 1)
            ).astype(BF16)
            dst[HALF:ROWS, 128 * t : 128 * t + 128] = jnp.where(
                low, pltpu.roll(a, 64, 1), b
            ).astype(BF16)

    cmat = call.at[d]
    assemble(4, cmat)
    x0 = pl.multiple_of(c * HALF, HALF)
    quarter = HALF // 2

    def c_copy(idx, recv):
        e = (d + ((3, 1, 2, 2)[idx] if recv else (0, 0, 3, 1)[idx])) % 4
        rows = (
            pl.ds(x0, HALF),
            pl.ds(x0, HALF),
            pl.ds(x0, quarter),
            pl.ds(x0 + quarter, quarter),
        )[idx]
        ref = call.at[e, rows]
        return rcopy(ref, ref, c_send.at[idx], c_recv.at[idx], dom((1, 3)[idx % 2]))

    def c_pass(o, recv):
        start = pl.multiple_of((1 - c) * HALF, HALF) if recv else x0
        ref = call.at[(d + o) % 4, pl.ds(start, HALF)]
        return rcopy(ref, ref, cs_send.at[o - 1], cs_recv.at[o - 1], sibling)

    c_copy(0, False).start()
    c_copy(1, False).start()
    for n in (0, 2):
        mix_pass(n + c).wait_recv()
        mix_pass(n + c).start()

    def reads(e):
        mine = par[pl.ds(pl.multiple_of(e * LP, LP), LP), :]

        cval = call[e].reshape(STEPS, LP, LANES)
        lhs = []
        for n in range(LP):
            q = (d * LP + n).astype(F32)
            mask = jnp.where(mine == q, 1.0, 0.0).astype(BF16)
            lhs.append((cval * mask[None]).reshape(ROWS, LANES))
        return lax.dot_general(
            jnp.concatenate(lhs, 1), sbf[...], NT, preferred_element_type=F32
        )

    start_read = reads(d)
    for idx, o in ((0, 3), (1, 1)):
        c_copy(idx, True).wait_recv()
        c_copy(2 + idx, False).start()
        c_pass(o, False).start()
    def u_half(top):
        rows = pl.ds(0 if top else HALF, HALF)
        n = 0 if top else 1
        return rcopy(
            ufar.at[rows], ufarr.at[rows], u_send.at[n], u_recv.at[n], dom(1 if top else 3)
        )

    def u_full(n, top):
        rows = pl.ds(0 if top else HALF, HALF)
        m = 2 + 2 * n + (0 if top else 1)
        return rcopy(
            usend.at[n, rows], urecv.at[n, rows], u_send.at[m], u_recv.at[m], dom(1 + 2 * n)
        )

    c_pass(1, True).wait_recv()
    usend[0] = reads((d + 1) % 4).astype(BF16)
    u_full(0, False).start()
    c_pass(3, True).wait_recv()
    usend[1] = reads((d + 3) % 4).astype(BF16)
    u_full(1, True).start()
    c_copy(2, True).wait_recv()
    c_copy(3, True).wait_recv()
    c_pass(2, False).start()
    gact = silu(acc[:, 0:256] * inv)
    c_pass(2, True).wait_recv()
    ufar[...] = reads((d + 2) % 4).astype(BF16)
    u_half(True).start()
    u_half(False).start()
    for n in (0, 2):
        mix_pass(n + 1 - c).wait_recv()
    assemble(0, bmat)
    gram = lax.dot_general(cmat[...], bmat[...], NT, preferred_element_type=F32)
    u_half(True).wait_recv()
    usend[0, 0:HALF] = usend[0, 0:HALF] + ufarr[0:HALF]
    u_full(0, True).start()
    u_half(False).wait_recv()
    usend[1, HALF:ROWS] = usend[1, HALF:ROWS] + ufarr[HALF:ROWS]
    u_full(1, False).start()

    sv = vact * spread(step)
    for h in range(4):
        inside = (lane >= 64 * h) & (lane < 64 * h + 64)
        sv4[h * ROWS : (h + 1) * ROWS, :] = jnp.where(inside, sv, 0.0).astype(BF16)
    gi = lax.broadcasted_iota(jnp.int32, (ROWS, ROWS), 0)
    gj = lax.broadcasted_iota(jnp.int32, (ROWS, ROWS), 1)
    keep = ((gi % LP) == (gj % LP)) & (gj <= gi)
    for h in range(4):
        diff = jnp.where(keep, run[:, 64 + h : 65 + h] - run_t[64 + h : 65 + h, :], -1e30)
        m4[:, h * ROWS : (h + 1) * ROWS] = (gram * jnp.exp(diff)).astype(BF16)
    inner = jnp.dot(m4[...], sv4[...], preferred_element_type=F32)
    inner = inner + spread(skip[...], 0) * vact
    carry = spread(jnp.exp(run))
    for n in range(2):
        for top in (True, False):
            u_full(n, top).wait_recv()
    start_read = start_read + urecv[0].astype(F32) + urecv[1].astype(F32)
    total = (inner + carry * start_read) * gact
    sq = lax.dot_general(
        jnp.ones((8, LANES), F32),
        total * total,
        NT,
        preferred_element_type=F32,
        precision=lax.Precision.HIGHEST,
    )
    place8 = me % 8
    sqs[place8] = sq

    def sq_copy(o):
        at = (place8 + o) % 8
        return rcopy(
            sqs.at[place8], sqs.at[place8], q_send.at[o - 1], q_recv.at[o - 1], {"head": z * 8 + at}
        )

    for o in range(1, 8):
        sq_copy(o).start()
    scaled[...] = (total * ogain[...]).astype(BF16)

    loads[10].wait()

    def terms(slot):
        return jnp.dot(
            scaled[...],
            wout[:, pl.ds(pl.multiple_of(slot * 256, 256), 256)],
            preferred_element_type=F32,
        )

    def sib_terms(n):
        return rcopy(sbuf.at[n], rbuf.at[n], rs_send.at[n], rs_recv.at[n], sibling)

    def give(*blocks):
        made = [terms(slot_sib(i, k)).astype(BF16) for i, k in blocks]
        for (i, k), block in zip(blocks, made):
            sbuf[i * 4 + k] = block
        for i, k in blocks:
            sib_terms(i * 4 + k).start()

    give((3, 3), (2, 3))
    give((1, 3), (0, 3))

    @pl.loop(0, 4)
    def _(t):
        give((3 - t, 1), (3 - t, 2))

    for o in range(1, 8):
        at = (place8 + 8 - o) % 8
        rcopy(sqs.at[at], sqs.at[at], q_send.at[o - 1], q_recv.at[o - 1], sibling).wait_recv()
    tsq = sqs[0]
    for o in range(1, 8):
        tsq = tsq + sqs[o]
    inv2 = lax.rsqrt(tsq.T[:, 0:1] / 2048.0 + 1e-5)
    inv2s[...] = jnp.broadcast_to(inv2, (ROWS, LANES))

    def finish(own, i, k):
        sib_terms(i * 4 + k).wait_recv()
        return (own + rbuf[i * 4 + k].astype(F32)) * inv2s[...]

    def half_copy(i, top, to):
        rows = pl.ds(0 if top else HALF, HALF)
        n = 0 if top else 1
        return rcopy(hsend.at[i, rows], hrecv.at[i, rows], r_send.at[i, n], r_recv.at[i, n], to)

    def full_copy(i, n, to):
        return rcopy(
            fsend.at[2 * i + n], frecv.at[2 * i + n], r_send.at[i, 2 + n], r_recv.at[i, 2 + n], to
        )

    @pl.loop(0, 4)
    def _(t):
        i = 3 - t
        hsend[i] = finish(terms(slot_own(i, 3)), i, 3).astype(BF16)
        half_copy(i, True, next2).start()
        half_copy(i, False, prev2).start()

    @pl.loop(0, 4)
    def _(t):
        i = 3 - t
        a = terms(slot_own(i, 1))
        b = terms(slot_own(i, 2))
        give((i, 0),)
        a = finish(a, i, 1)
        half_copy(i, True, next2).wait_recv()
        fsend[2 * i, 0:HALF] = (a[0:HALF] + hrecv[i, 0:HALF].astype(F32)).astype(BF16)
        fsend[2 * i, HALF:ROWS] = a[HALF:ROWS].astype(BF16)
        full_copy(i, 0, next2).start()
        b = finish(b, i, 2)
        half_copy(i, False, prev2).wait_recv()
        fsend[2 * i + 1, 0:HALF] = b[0:HALF].astype(BF16)
        fsend[2 * i + 1, HALF:ROWS] = (
            b[HALF:ROWS] + hrecv[i, HALF:ROWS].astype(F32)
        ).astype(BF16)
        full_copy(i, 1, prev2).start()

    @pl.loop(0, 4)
    def _(t):
        i = 3 - t
        rsum[i] = finish(terms(slot_own(i, 0)), i, 0)

    def column(i):
        full_copy(i, 0, next2).wait_recv()
        full_copy(i, 1, prev2).wait_recv()
        return rsum[i] + frecv[2 * i].astype(F32) + frecv[2 * i + 1].astype(F32)

    hsend[4] = column(3).astype(BF16)
    half_copy(4, True, next1).start()
    half_copy(4, False, prev1).start()

    def last_copy(n, top):
        rows = pl.ds(0 if top else HALF, HALF)
        m = 2 + 2 * n + (0 if top else 1)
        return rcopy(
            fsend.at[8 + n, rows],
            frecv.at[8 + n, rows],
            r_send.at[4, m],
            r_recv.at[4, m],
            (next1, prev1)[n],
        )

    b = column(2)
    fsend[9, 0:HALF] = b[0:HALF].astype(BF16)
    last_copy(1, True).start()
    a = column(1)
    fsend[8, HALF:ROWS] = a[HALF:ROWS].astype(BF16)
    last_copy(0, False).start()
    half_copy(4, True, next1).wait_recv()
    fsend[8, 0:HALF] = (a[0:HALF] + hrecv[4, 0:HALF].astype(F32)).astype(BF16)
    last_copy(0, True).start()
    half_copy(4, False, prev1).wait_recv()
    fsend[9, HALF:ROWS] = (b[HALF:ROWS] + hrecv[4, HALF:ROWS].astype(F32)).astype(BF16)
    last_copy(1, False).start()
    a = column(0)
    for n in range(2):
        for top in (True, False):
            last_copy(n, top).wait_recv()
    out_ref[...] = a + frecv[8].astype(F32) + frecv[9].astype(F32)

    for grp in range(5):
        for idx in range(6):
            ring(grp, idx, False).wait_send()

    @pl.loop(0, 16)
    def _(n):
        to_sib(n // 4, n % 4).wait_send()
        sib_terms(n).wait_send()

    @pl.loop(0, 4)
    def _(n):
        @pl.when(first + 2 * n != me)
        def _():
            mix_copy(n).wait_send()

        mix_pass(2 * n + c).wait_send()

    for idx in range(4):
        c_copy(idx, False).wait_send()
    for o in (1, 2, 3):
        c_pass(o, False).wait_send()
    for flag in (0, 1):
        u_half(flag == 0).wait_send()
        u_full(flag, True).wait_send()
        u_full(flag, False).wait_send()
    for o in range(1, 8):
        sq_copy(o).wait_send()
    for i in range(5):
        nxt, prv = (next1, prev1) if i == 4 else (next2, prev2)
        half_copy(i, True, nxt).wait_send()
        half_copy(i, False, prv).wait_send()
        if i == 4:
            for n in range(2):
                last_copy(n, True).wait_send()
                last_copy(n, False).wait_send()
        else:
            full_copy(i, 0, nxt).wait_send()
            full_copy(i, 1, prv).wait_send()


def body(
    tokens,
    parents,
    state,
    vhist,
    mhist,
    gain,
    gvw,
    mw,
    sw,
    vk,
    vo,
    mk,
    mo,
    so,
    dlog,
    skip,
    ogain,
    ow,
):
    v = gvw.reshape(8192, 2, 2, 128).transpose(0, 2, 1, 3).reshape(32768, 128)

    vmem = pl.BlockSpec(memory_space=pltpu.VMEM)
    hbm = pl.BlockSpec(memory_space=pl.ANY)
    dma = pltpu.SemaphoreType.DMA
    big = (ROWS, LANES)
    out = pl.pallas_call(
        kernel,
        out_shape=jax.ShapeDtypeStruct(big, F32),
        in_specs=[hbm] * 18,
        out_specs=vmem,
        scratch_shapes=[
            pltpu.VMEM((1, 64), jnp.int32),
            pltpu.VMEM((48, 256), F32),
            pltpu.VMEM((48, 64), F32),
            pltpu.VMEM((1, 256), F32),
            pltpu.VMEM((4, 256), F32),
            pltpu.VMEM((1, 256), F32),
            pltpu.VMEM((4, 64), F32),
            pltpu.VMEM((1, 64), F32),
            pltpu.VMEM((1, 4), F32),
            pltpu.VMEM((1, 4), F32),
            pltpu.VMEM((1, 4), F32),
            pltpu.VMEM((1, 256), F32),
            pltpu.VMEM((4, 8192), BF16),
            pltpu.VMEM((64, LANES), F32),
            pltpu.VMEM((32, TROWS, LANES), BF16),
            pltpu.VMEM((32768, 128), BF16),
            pltpu.VMEM((2, 512, 128), F32),
            pltpu.VMEM((8192, 512), BF16),
            pltpu.VMEM((128, 8192), BF16),
            pltpu.VMEM((256, 8192), BF16),
            pltpu.VMEM((LP, 256, 256), F32),
            pltpu.VMEM((256, LP * 256), BF16),
            pltpu.VMEM((ROWS, 512), F32),
            pltpu.VMEM((ROWS, 128), F32),
            pltpu.VMEM((ROWS, 128), F32),
            pltpu.VMEM((4, 48, 384), BF16),
            pltpu.VMEM((HALF, 128), BF16),
            pltpu.VMEM((8, HALF, 128), BF16),
            pltpu.VMEM(big, BF16),
            pltpu.VMEM((4, *big), BF16),
            pltpu.VMEM(big, BF16),
            pltpu.VMEM(big, BF16),
            pltpu.VMEM((2, *big), BF16),
            pltpu.VMEM((2, *big), BF16),
            pltpu.VMEM((4 * ROWS, LANES), BF16),
            pltpu.VMEM((ROWS, 4 * ROWS), BF16),
            pltpu.VMEM((8, 8, ROWS), F32),
            pltpu.VMEM(big, BF16),
            pltpu.VMEM(big, F32),
            pltpu.VMEM((16, *big), BF16),
            pltpu.VMEM((16, *big), BF16),
            pltpu.VMEM((5, *big), BF16),
            pltpu.VMEM((5, *big), BF16),
            pltpu.VMEM((10, *big), BF16),
            pltpu.VMEM((10, *big), BF16),
            pltpu.VMEM((4, *big), F32),
            dma((11,)),
            dma((14,)),
            dma((5, 6)),
            dma((5, 6)),
            dma((16,)),
            dma((16,)),
            dma((3,)),
            dma((3,)),
            dma((4,)),
            dma((8,)),
            dma((8,)),
            dma((4,)),
            dma((4,)),
            dma((3,)),
            dma((3,)),
            dma((6,)),
            dma((6,)),
            dma((7,)),
            dma((7,)),
            dma((5, 6)),
            dma((5, 6)),
            dma((16,)),
            dma((16,)),
        ],
        compiler_params=pltpu.CompilerParams(
            collective_id=0,
            has_side_effects=True,
            vmem_limit_bytes=63 * 1024 * 1024,
        ),
    )(
        tokens.reshape(ROWS, LANES),
        parents.reshape(1, 64),
        vhist.transpose(1, 0, 2).reshape(48, LANES),
        mhist.transpose(1, 0, 2).reshape(48, 64),
        gain.reshape(1, LANES),
        vk,
        vo.reshape(1, LANES),
        mk,
        mo.reshape(1, 64),
        so.reshape(1, 4),
        dlog.reshape(1, 4),
        skip.reshape(1, 4),
        ogain.reshape(1, LANES),
        sw.T,
        v,
        mw.T,
        ow,
        state.reshape(LP, 256, 256),
    )
    return out.astype(BF16).reshape(STEPS, LP, LANES)


def solution(mesh):
    return jax.shard_map(
        body,
        mesh=mesh,
        in_specs=(
            P(None, "dom", "head"),
            P(),
            P("dom", "head", None, None),
            P("dom", None, "head"),
            P("dom", None, "head"),
            P("head"),
            P(None, None, "head"),
            P(None, "head"),
            P(None, "head"),
            P(None, "head"),
            P("head"),
            P(None, "head"),
            P("head"),
            P("head"),
            P("head"),
            P("head"),
            P("head"),
            P("head", None),
        ),
        out_specs=P(None, "dom", "head"),
        check_vma=False,
    )
```
